128 devices in a mesh: lev: 8 (over y, core), row: 16 (over z, x).
Axes of the slice: x: 4, y: 4, z: 4, core: 2. Of those that a mesh axis runs over, the one named last changes fastest.
Arguments:
- tracer: float32 [128, 64, 4096], P('lev', 'row'), may hold values from -6 to 6
- courant_x: float32 [128, 64, 4096], P('lev', 'row'), may hold values from 0.05 to 0.45
- courant_y: float32 [128, 64, 4096], P('lev', 'row'), may hold values from 0.05 to 0.45
- wind_x: int32 [128, 64, 4096], P('lev', 'row'), may hold values 0 or 1
- wind_y: int32 [128, 64, 4096], P('lev', 'row'), may hold values 0 or 1
- inverse_diffusion: float32 [4096, 128, 128], P(('lev', 'row')), may hold values from -0.5 to 1.5
- receptor_cell: int32 [262144], P(('lev', 'row')), may hold values from 0 to 262143
- receptor_limit: float32 [262144], P(('lev', 'row')), may hold values from -1 to 1
- stack_cell: int32 [65536], P(('lev', 'row')), may hold values from 0 to 262143
- stack_dest: int32 [65536, 1], P(('lev', 'row')), may hold values from 0 to 127; in each aligned block of 512 rows (0 to 511, 512 to 1023, ...) at most 12 rows name the same one
- stack_slot: int32 [65536], P(('lev', 'row')), may hold values from 0 to 255
- stack_weight: float32 [65536], P(('lev', 'row')), may hold values from 0.5 to 2
Outputs:
- final_field: float32 [4096, 64, 128], P(('lev', 'row'))
- crossing: float32 [262144], P(('lev', 'row'))
- adjoint_init: float32 [128, 64, 4096], P('lev', 'row')
- inventory_grad: float32 [32768], P(('lev', 'row'))
The draws below stay inside these ranges and needn't reach their ends.
Inputs may be any that keep to these rules, and one draw needn't show every extreme that they name: `stack_dest`: among the stacks of one slab strip at most 12 have the same owner.
All inputs are finite; a program needn't handle non-finite values. No bound on the sum of `wind_x` or of `wind_y` on one device may be relied on, other than what follows from the above.
Results may differ from the reference program's by a relative error of at most 0.00011.
Values sent between devices are 32-bit elements; how exact they have to be, the bound alone decides.
A program may use at most 128 MiB of HBM per device.

```python
import math
import jax
import jax.numpy as jnp
import numpy as np
from jax import lax

L = 128
NY = 4096
RX = 4
REC_DEV = 2048
S_DEV = 512
INV_DEV = 256
NX = 64
LS = 16
YC = 32
CAP = 12
RECEPTORS = 262144
STACKS = 65536
INVENTORY = 32768
N_LEV = 8
N_ROW = 16


def draw_inverse_diffusion(key, part):
    key_diagonal, key_spread = jax.random.split(key)
    diagonal = jax.random.uniform(key_diagonal, (NY, L), jnp.float32, 0.5, 1.0)
    spread_part = jnp.clip(jax.random.normal(key_spread, (NY, L, L), jnp.float32), -4.0, 4.0) * 0.5 / math.sqrt(L)
    identity = jnp.eye(L, dtype=jnp.float32)
    return identity[None, :, :] * diagonal[:, :, None] + spread_part


def set_ends(values, stream_key, least, top_value):
    longest = values.shape.index(max(values.shape))
    spots = []
    for shift in (0, 1):
        where = [jax.random.randint(jax.random.fold_in(stream_key, axis), (), 0, length) for axis, length in enumerate(values.shape)]
        where[longest] = (where[longest] + shift) % values.shape[longest]
        spots.append(tuple(where))
    return values.at[spots[0]].set(least).at[spots[1]].set(top_value)


def level_of(rng, dims, pieces, least, high):
    factor_of = 1.0
    for dim, parts in pieces:
        heights = jax.random.uniform(jax.random.fold_in(jax.random.fold_in(rng, 6), dim), (parts,), jnp.float32, least / len(pieces), high / len(pieces))
        factor_of = factor_of * jnp.repeat(jnp.exp(heights), dims[dim] // parts).reshape((-1,) + (1,) * (len(dims) - 1 - dim))
    return factor_of


def assign_block(own_key, own, number, rows, count, top, reach, lean):
    order = jax.random.permutation(own_key, count)
    heavy_load, usual = portions_of(count, rows * top, reach, lean, True), portions_of(count, rows * top, reach, lean, False)
    places = jnp.arange(count)

    def named(lengths, offset_by):
        used = int((lengths > 0).sum())
        fixed = max(1, used // 4)
        moved = fixed + (places - fixed + offset_by * (used - fixed)) % max(1, count - fixed)
        return jnp.zeros((count,), jnp.int32).at[order[jnp.where(places < fixed, places, moved)]].set(jnp.asarray(lengths, jnp.int32))

    lengths = jnp.where(number % 4 == 0, named(heavy_load, number // 4), named(usual, number - number // 4 - 1))
    mixed = jax.random.permutation(jax.random.fold_in(own, 3), count)
    source_of, taker = mixed[0:count // 2 * 2:2], mixed[1:count // 2 * 2:2]
    room = jnp.minimum(lengths[source_of] - 1, reach - lengths[taker]) // 2
    room = jnp.where((source_of == order[0]) | (taker == order[0]) | (lengths[taker] == 0), 0, jnp.maximum(room, 0))
    moved = jax.random.randint(jax.random.fold_in(own, 4), (count // 2,), 0, 1 << 20) % (room + 1)
    lengths = lengths.at[source_of].add(-moved).at[taker].add(moved)
    members = jnp.searchsorted(jnp.cumsum(lengths), jnp.arange(rows * top), side="right").astype(jnp.int32)
    grid = members.reshape(top, rows).T
    grid = grid[jax.random.permutation(jax.random.fold_in(own, 1), rows)]
    offset_by = jax.random.randint(jax.random.fold_in(own, 2), (rows, 1), 0, top)
    return jnp.take_along_axis(grid, (jnp.arange(top)[None, :] + offset_by) % top, axis=1)


def portions_of(amount, total, most, slope, full):
    loads = [(1 << 20) // math.isqrt(rank ** slope) + 1 for rank in range(1, amount + 1)]
    largest = most if full else min(most, max(-(-total // amount), total * loads[0] // sum(loads)))
    least = 1 if total - largest >= amount - 1 else 0
    counts, rest = [largest] + [least] * (amount - 1), total - largest - least * (amount - 1)
    while rest > 0:
        free = [i for i in range(1, amount) if counts[i] < largest] or [i for i in range(1, amount) if counts[i] < most]
        pool, left = sum([loads[i] for i in free]), rest
        for i in free:
            addition = min(most - counts[i], max(1, left * loads[i] // pool), rest)
            counts[i] = counts[i] + addition
            rest = rest - addition
    return np.array(counts)


def centred(own_key, dims, spread, reach, shards=(), held_as=jnp.bfloat16):
    result = spread * jax.random.normal(own_key, dims, jnp.float32)
    if shards:
        result = result * level_of(own_key, dims, shards, -0.22, 0.18)
    return jnp.clip(result, -reach, reach).astype(held_as)


def setup_inputs(seed: int = 0) -> dict:
    arg_keys = jax.random.split(jax.random.key(seed), 13)
    tracer = centred(arg_keys[0], (L, NX, NY), 1.0, 6.0, ((0, 8), (1, 16)), jnp.float32)
    courant_x = jnp.clip(jnp.exp(math.log(0.45) - 2.1972245 * jax.random.uniform(arg_keys[1], (L, NX, NY), jnp.float32) ** level_of(arg_keys[1], (L, NX, NY), ((0, 8), (1, 16)), -0.2, 0.2)), 0.05, 0.45)
    courant_y = jnp.clip(jnp.exp(math.log(0.45) - 2.1972245 * jax.random.uniform(arg_keys[2], (L, NX, NY), jnp.float32) ** level_of(arg_keys[2], (L, NX, NY), ((0, 8), (1, 16)), -0.2, 0.2)), 0.05, 0.45)
    wind_x = set_ends((jax.random.randint(arg_keys[3], (L, NX, NY), 0, 2) < 1).astype(jnp.int32), jax.random.fold_in(arg_keys[3], 1), 0, 1)
    wind_y = set_ends((jax.random.randint(arg_keys[4], (L, NX, NY), 0, 2) < 1).astype(jnp.int32), jax.random.fold_in(arg_keys[4], 1), 0, 1)
    inverse_diffusion = draw_inverse_diffusion(jax.random.fold_in(arg_keys[12], 71), 0)
    receptor_cell = set_ends(jax.random.randint(arg_keys[6], (RECEPTORS,), 0, YC * NX * L), jax.random.fold_in(arg_keys[6], 1), 0, (YC * NX * L) - 1).astype(jnp.int32)
    receptor_limit = jnp.clip(jax.random.uniform(arg_keys[7], (RECEPTORS,), jnp.float32, -1.0, 1.0) * level_of(arg_keys[7], (RECEPTORS,), ((0, 128),), -0.4, 0.0), -1.0, 1.0)
    stack_cell = set_ends(jax.random.randint(arg_keys[8], (STACKS,), 0, LS * RX * NY), jax.random.fold_in(arg_keys[8], 1), 0, (LS * RX * NY) - 1).astype(jnp.int32)
    stack_dest_keys = jax.random.split(jax.random.fold_in(arg_keys[9], 1), STACKS // S_DEV)
    stack_dest_turns = jax.random.permutation(jax.random.fold_in(arg_keys[9], 3), STACKS // S_DEV)
    stack_dest = jax.vmap(lambda own, number: assign_block(jax.random.fold_in(arg_keys[9], 2), own, number, S_DEV, N_LEV * N_ROW, 1, CAP, 2))(stack_dest_keys, stack_dest_turns).reshape((STACKS, 1))
    stack_slot = set_ends(jax.random.randint(arg_keys[10], (STACKS,), 0, INV_DEV), jax.random.fold_in(arg_keys[10], 1), 0, INV_DEV - 1).astype(jnp.int32)
    stack_weight = jnp.clip(jnp.exp(math.log(2.0) - 1.3862944 * jax.random.uniform(arg_keys[11], (STACKS,), jnp.float32) ** level_of(arg_keys[11], (STACKS,), ((0, 128),), -0.2, 0.2)), 0.5, 2.0)
    return dict(tracer=tracer, courant_x=courant_x, courant_y=courant_y, wind_x=wind_x, wind_y=wind_y, inverse_diffusion=inverse_diffusion, receptor_cell=receptor_cell, receptor_limit=receptor_limit, stack_cell=stack_cell, stack_dest=stack_dest, stack_slot=stack_slot, stack_weight=stack_weight)


SHARPNESS = 2.0

def advect(field, courant_x, courant_y, sign_x, sign_y):
    padded = jnp.pad(field, ((0, 0), (1, 1), (1, 1)))
    lower_x = padded[:, :-2, 1:-1]
    upper_x = padded[:, 2:, 1:-1]
    lower_y = padded[:, 1:-1, :-2]
    upper_y = padded[:, 1:-1, 2:]
    return (1.0 - courant_x - courant_y) * field + courant_x * (sign_x * lower_x + (1.0 - sign_x) * upper_x) + courant_y * (sign_y * lower_y + (1.0 - sign_y) * upper_y)

def reference(tracer, courant_x, courant_y, wind_x, wind_y, inverse_diffusion, receptor_cell, receptor_limit, stack_cell, stack_dest, stack_slot, stack_weight):
    sign_x = wind_x.astype(jnp.float32)
    sign_y = wind_y.astype(jnp.float32)
    advected = advect(tracer, courant_x, courant_y, sign_x, sign_y)
    columns = jnp.transpose(advected, (2, 1, 0))
    final_field = jnp.einsum('yxk,ylk->yxl', columns, inverse_diffusion, precision=lax.Precision.HIGHEST)
    block_size = YC * NX * L
    owner_block = jnp.arange(RECEPTORS, dtype=jnp.int32) // REC_DEV
    flat_index = owner_block * block_size + receptor_cell
    picked = final_field.reshape(-1)[flat_index]
    crossing = jax.nn.sigmoid(SHARPNESS * (picked - receptor_limit))
    seed_terms = SHARPNESS * crossing * (1.0 - crossing)
    seed_field = jnp.zeros((NY * NX * L,), jnp.float32).at[flat_index].add(seed_terms).reshape(NY, NX, L)
    back_mid = jnp.einsum('yxl,ylk->yxk', seed_field, inverse_diffusion, precision=lax.Precision.HIGHEST)
    back_slab = jnp.transpose(back_mid, (2, 1, 0))
    _, pullback = jax.vjp(lambda field: advect(field, courant_x, courant_y, sign_x, sign_y), tracer)
    adjoint_init = pullback(back_slab)[0]
    strip = jnp.arange(STACKS, dtype=jnp.int32) // S_DEV
    lev_index = strip // N_ROW
    row_index = strip % N_ROW
    level = lev_index * LS + stack_cell // (RX * NY)
    row_pos = row_index * RX + stack_cell // NY % RX
    col_pos = stack_cell % NY
    stack_values = stack_weight * adjoint_init[level, row_pos, col_pos]
    owner = stack_dest[:, 0] * INV_DEV + stack_slot
    inventory_grad = jnp.zeros((INVENTORY,), jnp.float32).at[owner].add(stack_values)
    return (final_field, crossing, adjoint_init, inventory_grad)
```

```python
import functools

import jax
import jax.numpy as jnp
from jax import lax
from jax.experimental import pallas as pl
from jax.experimental.pallas import tpu as pltpu
from jax.sharding import PartitionSpec as P

F32 = jnp.float32
BF16 = jnp.bfloat16
I32 = jnp.int32
MESH = pl.DeviceIdType.MESH
N_LEV = 8
N_ROW = 16
N = N_LEV * N_ROW
ROWS = 2048
REC_TILE = 512


def place(d):
    return (d // N_ROW, lax.rem(d, N_ROW))


def iota(shape, dim):
    return lax.broadcasted_iota(I32, shape, dim)


def swap4(v, unit):
    lane = iota(v[0].shape, 1)
    for bit in (1, 2):
        step = unit * bit
        high = (lane & step) != 0
        out = list(v)
        for a in range(4):
            if a & bit:
                continue
            b = a | bit
            out[a] = jnp.where(high, pltpu.roll(v[b], step, 1), v[a])
            out[b] = jnp.where(high, v[b], pltpu.roll(v[a], 128 - step, 1))
        v = out
    return v


def as_column(row):
    return jnp.broadcast_to(row, (128, 128)).T


def as_row(column):
    eye = iota((128, 128), 0) == iota((128, 128), 1)
    return jnp.sum(jnp.where(eye, jnp.broadcast_to(column, (128, 128)), 0.0), axis=0, keepdims=True)


def halves(v):
    high = v.astype(BF16)
    return high, (v - high.astype(F32)).astype(BF16)


def dot(a, b, dims):
    return lax.dot_general(a, b, (dims, ((), ())), preferred_element_type=F32)


def dot3(a, b, dims):
    ah, al = halves(a)
    bh, bl = halves(b)
    return dot(ah, bh, dims) + (dot(ah, bl, dims) + dot(al, bh, dims))


def one_hot(mask):
    return jnp.where(mask, 1.0, 0.0).astype(BF16)


def kernel(
    t_in, cx_in, cy_in, sx_in, sy_in, mat_in, rcell, rlim, scell, sdest, sslot, swt,
    final_out, cross_out, adj_out, inv_out,
    t, cx, cy, sx, sy, mat, work, cols, field, parts, hot, values, send_a, recv_a, recv_b, send_c, recv_c,
    halo_send, halo_recv, hback_send, hback_recv, picked,
    load_sem, own_sem, out_sem, hs_sem, hr_sem, as_sem, ar_sem, bs_sem, br_sem, cs_sem, cr_sem,
):
    my_lev = lax.axis_index("lev")
    my_row = lax.axis_index("row")
    me = my_lev * N_ROW + my_row
    up_row = lax.rem(my_row + 1, N_ROW)
    down_row = lax.rem(my_row + N_ROW - 1, N_ROW)

    loads = []
    for n, (src, dst) in enumerate(((t_in, t), (cx_in, cx), (cy_in, cy), (sx_in, sx), (sy_in, sy), (mat_in, mat))):
        c = pltpu.make_async_copy(src, dst, load_sem.at[n])
        c.start()
        loads.append(c)

    barrier = pltpu.get_barrier_semaphore()

    @pl.loop(1, N)
    def _(k):
        pl.semaphore_signal(barrier, inc=1, device_id=place(lax.rem(me + k, N)), device_id_type=MESH)

    loads[0].wait()
    halo_send[0] = t[pl.ds(3, 512, stride=4), :]
    halo_send[1] = t[pl.ds(0, 512, stride=4), :]
    pl.semaphore_wait(barrier, N - 1)

    def exchange(send, recv, rows, slot):
        c = pltpu.make_async_remote_copy(
            send.at[slot], recv.at[slot], hs_sem.at[rows + slot], hr_sem.at[rows + slot],
            device_id=(my_lev, (up_row, down_row)[slot]), device_id_type=MESH,
        )
        c.start()
        return c

    halo = [exchange(halo_send, halo_recv, 0, s) for s in (0, 1)]
    for c in loads[1:5]:
        c.wait()

    tile_row = iota((128, 128), 0)
    tile_lane = iota((128, 128), 1)
    strip_row = tile_row & 3

    def from_left(v):
        rolled = pltpu.roll(v, 1, 1)
        carried = jnp.where(tile_row < 4, 0.0, pltpu.roll(rolled, 4, 0))
        return jnp.where(tile_lane == 0, carried, rolled)

    def from_right(v):
        rolled = pltpu.roll(v, 127, 1)
        carried = jnp.where(tile_row >= 124, 0.0, pltpu.roll(rolled, 124, 0))
        return jnp.where(tile_lane == 127, carried, rolled)

    def from_before(v):
        return jnp.where(strip_row == 0, 0.0, pltpu.roll(v, 1, 0))

    def from_after(v):
        return jnp.where(strip_row == 3, 0.0, pltpu.roll(v, 127, 0))

    @pl.loop(0, 16)
    def _(lev):
        at = pl.ds(pl.multiple_of(lev * 128, 128), 128)
        v, a, b = t[at], cx[at], cy[at]
        work[at] = (
            (1.0 - a - b) * v
            + a * jnp.where(sx[at] != 0, from_before(v), from_after(v))
            + b * jnp.where(sy[at] != 0, from_left(v), from_right(v))
        )

    first = pl.ds(0, 512, stride=4)
    final = pl.ds(3, 512, stride=4)
    for c in halo:
        c.wait()
    has_down = jnp.where(my_row > 0, 1.0, 0.0)
    has_up = jnp.where(my_row < N_ROW - 1, 1.0, 0.0)
    work[first, :] = work[first, :] + has_down * jnp.where(sx[first, :] != 0, cx[first, :] * halo_recv[0], 0.0)
    work[final, :] = work[final, :] + has_up * jnp.where(sx[final, :] != 0, 0.0, cx[final, :] * halo_recv[1])

    low = iota((8, 128), 0) < 4
    here = my_row * N_LEV + my_lev

    @pl.loop(0, 16)
    def _(k):
        pair = lax.rem(k + me // 8, 16)
        at = pl.multiple_of(pair * 8, 8)
        groups = []
        for group in range(4):
            v = [work[pl.ds(pl.multiple_of((group * 4 + g) * 128 + at, 8), 8), :] for g in range(4)]
            groups.append(swap4(v, 32))
        for half in range(2):
            for q in range(4):
                a, b = groups[half * 2][q], groups[half * 2 + 1][q]
                send_a[at + q, half * 8:half * 8 + 8] = jnp.where(low, a, pltpu.roll(b, 4, 0))
                send_a[at + 4 + q, half * 8:half * 8 + 8] = jnp.where(low, pltpu.roll(a, 4, 0), b)

        @pl.loop(0, 8)
        def _(e):
            @pl.when(k + e > 0)
            def _():
                other = at + lax.rem(e + me, 8)
                pltpu.make_async_remote_copy(
                    send_a.at[other], recv_a.at[here], as_sem, ar_sem, device_id=place(other), device_id_type=MESH
                ).start()

            @pl.when(k + e == 0)
            def _():
                pltpu.make_async_copy(send_a.at[me], recv_a.at[here], own_sem).start()

    def all_of(send, recv, ss, rs):
        return pltpu.make_async_remote_copy(
            send.at[pl.ds(0, N - 1)], recv.at[pl.ds(0, N - 1)], ss, rs,
            device_id=(my_lev, up_row), device_id_type=MESH,
        )

    loads[5].wait()
    pltpu.make_async_copy(send_a.at[me], recv_a.at[here], own_sem).wait()
    flow = all_of(send_a, recv_a, as_sem, ar_sem)
    flow.wait_recv()

    @pl.loop(0, 16)
    def _(j):
        v = recv_a[pl.ds(j * 8, 8)].reshape(128, 128).T
        for r, u in enumerate(swap4([v[g * 32:g * 32 + 32] for g in range(4)], 1)):
            cols[pl.ds(pl.multiple_of(j * 128 + r * 32, 32), 32), :] = u

    @pl.loop(0, 32)
    def _(y):
        v = dot3(cols[pl.ds(y, 64, stride=32), :], mat[y], ((1,), (1,)))
        at = pl.ds(pl.multiple_of(y * 64, 64), 64)
        field[at] = v
        h, l = halves(v)
        parts[at, 0:128] = h
        parts[at, 128:256] = l

    final_copy = pltpu.make_async_copy(field, final_out, out_sem.at[0])
    final_copy.start()

    lanes = iota((REC_TILE, 128), 1)

    def column(ref, base):
        return jnp.concatenate([as_column(ref(base + s)) for s in range(REC_TILE // 128)], axis=0)

    def pick(base, row_of, lane_of, out):
        rows = column(row_of, base)
        for k in range(16):
            hot[:, k * 128:k * 128 + 128] = one_hot(rows == lanes + k * 128)
        g = dot(hot[...], parts[...], ((1,), (0,)))
        g = g[:, :128] + g[:, 128:]
        g = jnp.sum(jnp.where(column(lane_of, base) == lanes, g, 0.0), axis=1, keepdims=True)
        for s in range(REC_TILE // 128):
            out[pl.ds(base + s, 1), :] = as_row(g[s * 128:s * 128 + 128])

    @pl.loop(0, 4)
    def _(u):
        pick(u * 4, lambda s: rcell[pl.ds(s, 1), :] >> 7, lambda s: rcell[pl.ds(s, 1), :] & 127, picked)

    crossing = jax.nn.sigmoid(2.0 * (picked[...] - rlim[...]))
    cross_out[...] = crossing
    picked[...] = 2.0 * crossing * (1.0 - crossing)

    @pl.loop(0, 16)
    def _(u):
        seeds = as_column(picked[pl.ds(u, 1), :])
        mask = as_column(rcell[pl.ds(u, 1), :] & 127) == tile_lane
        h, l = halves(jnp.where(mask, seeds, 0.0))
        at = pl.ds(pl.multiple_of(u * 128, 128), 128)
        values[at, 0:128] = h
        values[at, 128:256] = l

    @pl.loop(0, 4)
    def _(u):
        rows = iota((REC_TILE, 128), 0) + u * REC_TILE
        for k in range(16):
            hot[:, k * 128:k * 128 + 128] = one_hot((rcell[k:k + 1, :] >> 7) == rows)
        g = dot(hot[...], values[...], ((1,), (0,)))
        work[pl.ds(pl.multiple_of(u * REC_TILE, REC_TILE), REC_TILE), :] = g[:, :128] + g[:, 128:]

    @pl.loop(0, 32)
    def _(y):
        at = pl.ds(pl.multiple_of(y * 64, 64), 64)
        cols[pl.ds(y, 64, stride=32), :] = dot3(work[at], mat[y], ((1,), (0,)))

    flow.wait_send()

    @pl.loop(0, 16)
    def _(k):
        j = lax.rem(k + my_row, N_ROW)
        v = [cols[pl.ds(pl.multiple_of(j * 128 + r * 32, 32), 32), :] for r in range(4)]
        v = jnp.concatenate(swap4(v, 1), axis=0).T
        send_a[pl.ds(j * 8, 8)] = v.reshape(8, 16, 128)

        @pl.loop(0, 8)
        def _(e):
            i = lax.rem(e + my_lev, N_LEV)

            @pl.when(k + e > 0)
            def _():
                pltpu.make_async_remote_copy(
                    send_a.at[j * 8 + i], recv_b.at[me], bs_sem, br_sem, device_id=(i, j), device_id_type=MESH
                ).start()

            @pl.when(k + e == 0)
            def _():
                pltpu.make_async_copy(send_a.at[here], recv_b.at[me], own_sem).start()

    pltpu.make_async_copy(send_a.at[here], recv_b.at[me], own_sem).wait()
    flow = all_of(send_a, recv_b, bs_sem, br_sem)
    flow.wait_recv()

    @pl.loop(0, 16)
    def _(pair):
        at = pl.multiple_of(pair * 8, 8)
        for half in range(2):
            va, vb = [], []
            for q in range(4):
                p = recv_b[at + q, half * 8:half * 8 + 8]
                s = recv_b[at + 4 + q, half * 8:half * 8 + 8]
                va.append(jnp.where(low, p, pltpu.roll(s, 4, 0)))
                vb.append(jnp.where(low, pltpu.roll(p, 4, 0), s))
            for group, v in ((half * 2, va), (half * 2 + 1, vb)):
                for g, u in enumerate(swap4(v, 32)):
                    t[pl.ds(pl.multiple_of((group * 4 + g) * 128 + at, 8), 8), :] = u

    hback_send[0] = jnp.where(sx[final, :] != 0, 0.0, cx[final, :] * t[final, :])
    hback_send[1] = jnp.where(sx[first, :] != 0, cx[first, :] * t[first, :], 0.0)
    halo = [exchange(hback_send, hback_recv, 2, s) for s in (0, 1)]

    @pl.loop(0, 16)
    def _(lev):
        at = pl.ds(pl.multiple_of(lev * 128, 128), 128)
        v, a, b = t[at], cx[at], cy[at]
        flux_x, flux_y = a * v, b * v
        lower_x, lower_y = sx[at] != 0, sy[at] != 0
        work[at] = (
            (1.0 - a - b) * v
            + from_after(jnp.where(lower_x, flux_x, 0.0))
            + from_before(jnp.where(lower_x, 0.0, flux_x))
            + from_right(jnp.where(lower_y, flux_y, 0.0))
            + from_left(jnp.where(lower_y, 0.0, flux_y))
        )

    for c in halo:
        c.wait()
    work[first, :] = work[first, :] + has_down * hback_recv[0]
    work[final, :] = work[final, :] + has_up * hback_recv[1]
    adj_copy = pltpu.make_async_copy(work, adj_out, out_sem.at[1])
    adj_copy.start()

    @pl.loop(0, 16)
    def _(lev):
        at = pl.ds(pl.multiple_of(lev * 128, 128), 128)
        h, l = halves(work[at])
        parts[at, 0:128] = h
        parts[at, 128:256] = l

    def stack_row(s):
        c = scell[pl.ds(s, 1), :]
        return (c >> 14) * 128 + ((c >> 7) & 31) * 4 + ((c >> 12) & 3)

    pick(0, stack_row, lambda s: scell[pl.ds(s, 1), :] & 127, picked)
    stack_values = picked[0:4, :] * swt[...]
    partial = jnp.zeros((128, 256), F32)
    wide = iota((128, 256), 1)
    for s in range(4):
        owner = one_hot(sdest[s:s + 1, :] == tile_row)
        slot = as_column(sslot[s:s + 1, :])
        amount = as_column(stack_values[s:s + 1, :])
        slot = jnp.concatenate([slot, slot], axis=1)
        amount = jnp.concatenate([amount, amount], axis=1)
        h, l = halves(jnp.where(slot == wide, amount, 0.0))
        partial = partial + (dot(owner, h, ((1,), (0,))) + dot(owner, l, ((1,), (0,))))
    send_c[:, 0, :] = partial[:, :128]
    send_c[:, 1, :] = partial[:, 128:]

    @pl.loop(1, N)
    def _(k):
        other = lax.rem(me + k, N)
        pltpu.make_async_remote_copy(
            send_c.at[other], recv_c.at[me], cs_sem, cr_sem, device_id=place(other), device_id_type=MESH
        ).start()

    own = pltpu.make_async_copy(send_c.at[me], recv_c.at[me], own_sem)
    own.start()
    own.wait()
    last = all_of(send_c, recv_c, cs_sem, cr_sem)
    last.wait_recv()
    inv_out[...] = jnp.sum(recv_c[...], axis=0)
    last.wait_send()
    flow.wait_send()
    final_copy.wait()
    adj_copy.wait()


def rows_of(slab):
    return slab.reshape(16, 4, 32, 128).transpose(0, 2, 1, 3).reshape(ROWS, 128)


def local(
    tracer, courant_x, courant_y, wind_x, wind_y, inverse_diffusion,
    receptor_cell, receptor_limit, stack_cell, stack_dest, stack_slot, stack_weight,
):
    vmem = pl.BlockSpec(memory_space=pltpu.VMEM)
    hbm = pl.BlockSpec(memory_space=pl.ANY)
    slab = pltpu.VMEM((ROWS, 128), F32)
    dma = pltpu.SemaphoreType.DMA
    blocks = pltpu.VMEM((N, 16, 128), F32)
    edge = pltpu.VMEM((2, 512, 128), F32)
    final_field, crossing, adjoint, inventory = pl.pallas_call(
        kernel,
        out_shape=(
            jax.ShapeDtypeStruct((ROWS, 128), F32),
            jax.ShapeDtypeStruct((16, 128), F32),
            jax.ShapeDtypeStruct((ROWS, 128), F32),
            jax.ShapeDtypeStruct((2, 128), F32),
        ),
        in_specs=[hbm] * 6 + [vmem] * 6,
        out_specs=(hbm, vmem, hbm, vmem),
        scratch_shapes=[
            slab, slab, slab, pltpu.VMEM((ROWS, 128), I32), pltpu.VMEM((ROWS, 128), I32), pltpu.VMEM((32, 128, 128), F32),
            slab, slab, slab, pltpu.VMEM((ROWS, 256), BF16), pltpu.VMEM((REC_TILE, ROWS), BF16),
            pltpu.VMEM((ROWS, 256), BF16), blocks, blocks, blocks,
            pltpu.VMEM((N, 2, 128), F32), pltpu.VMEM((N, 2, 128), F32),
            edge, edge, edge, edge, pltpu.VMEM((16, 128), F32),
            dma((6,)), dma, dma((2,)), dma((4,)), dma((4,)), dma, dma, dma, dma, dma, dma,
        ],
        compiler_params=pltpu.CompilerParams(
            collective_id=0, has_side_effects=True, vmem_limit_bytes=56 * 1024 * 1024
        ),
        name="transport",
    )(
        rows_of(tracer), rows_of(courant_x), rows_of(courant_y), rows_of(wind_x), rows_of(wind_y), inverse_diffusion,
        receptor_cell.reshape(16, 128), receptor_limit.reshape(16, 128), stack_cell.reshape(4, 128),
        stack_dest.reshape(4, 128), stack_slot.reshape(4, 128), stack_weight.reshape(4, 128),
    )
    adjoint = adjoint.reshape(16, 32, 4, 128).transpose(0, 2, 1, 3).reshape(16, 4, 4096)
    return final_field.reshape(32, 64, 128), crossing.reshape(-1), adjoint, inventory.reshape(-1)


def solution(mesh):
    slab = P("lev", "row", None)
    flat = P(("lev", "row"))
    return jax.shard_map(
        local,
        mesh=mesh,
        in_specs=(slab,) * 5 + (P(("lev", "row"), None, None), flat, flat, flat, P(("lev", "row"), None), flat, flat),
        out_specs=(P(("lev", "row"), None, None), flat, slab, flat),
        check_vma=False,
    )
```

```python
import functools

import jax
import jax.numpy as jnp
from jax import lax
from jax.experimental import pallas as pl
from jax.experimental.pallas import tpu as pltpu
from jax.sharding import PartitionSpec as P

F32 = jnp.float32
BF16 = jnp.bfloat16
I32 = jnp.int32
MESH = pl.DeviceIdType.MESH
N_LEV = 8
N_ROW = 16
N = N_LEV * N_ROW
ROWS = 2048
REC_TILE = 512


def place(d):
    return (d // N_ROW, lax.rem(d, N_ROW))


def iota(shape, dim):
    return lax.broadcasted_iota(I32, shape, dim)


def swap4(v, unit):
    lane = iota(v[0].shape, 1)
    for bit in (1, 2):
        step = unit * bit
        high = (lane & step) != 0
        out = list(v)
        for a in range(4):
            if a & bit:
                continue
            b = a | bit
            out[a] = jnp.where(high, pltpu.roll(v[b], step, 1), v[a])
            out[b] = jnp.where(high, v[b], pltpu.roll(v[a], 128 - step, 1))
        v = out
    return v


def as_column(row):
    return jnp.broadcast_to(row, (128, 128)).T


def as_row(column):
    eye = iota((128, 128), 0) == iota((128, 128), 1)
    return jnp.sum(jnp.where(eye, jnp.broadcast_to(column, (128, 128)), 0.0), axis=0, keepdims=True)


def halves(v):
    high = v.astype(BF16)
    return high, (v - high.astype(F32)).astype(BF16)


def dot(a, b, dims):
    return lax.dot_general(a, b, (dims, ((), ())), preferred_element_type=F32)


def dot_split(a, b, dims):
    n = a.shape[0]
    side = 0 if dims[1] == (1,) else 1
    g = dot(jnp.concatenate(halves(a), axis=0), jnp.concatenate(halves(b), axis=side), dims)
    return (g[:n, :128] + g[n:, :128]) + (g[:n, 128:] + g[n:, 128:])


def one_hot(mask):
    return jnp.where(mask, 1.0, 0.0).astype(BF16)


def kernel(
    t_in, cx_in, cy_in, sx_in, sy_in, mat_in, rcell, rlim, scell, sdest, sslot, swt,
    final_out, cross_out, adj_out, inv_out,
    t, cx, cy, sx, sy, mat, work, cols, field, parts, hot, values, send_a, recv_a, recv_b, level_send, level_recv, row_send, row_recv,
    halo_send, halo_recv, hback_send, hback_recv, picked,
    load_sem, own_sem, out_sem, hs_sem, hr_sem, as_sem, ar_sem, bs_sem, br_sem, cs_sem, cr_sem, ready,
):
    my_lev = lax.axis_index("lev")
    my_row = lax.axis_index("row")
    me = my_lev * N_ROW + my_row
    up_row = lax.rem(my_row + 1, N_ROW)
    down_row = lax.rem(my_row + N_ROW - 1, N_ROW)

    loads = []
    for n, (src, dst) in enumerate(((t_in, t), (cx_in, cx), (cy_in, cy), (sx_in, sx), (sy_in, sy), (mat_in, mat))):
        c = pltpu.make_async_copy(src, dst, load_sem.at[n])
        c.start()
        loads.append(c)

    barrier = pltpu.get_barrier_semaphore()

    @pl.loop(1, N_ROW)
    def _(k):
        other = (my_lev, lax.rem(my_row + k, N_ROW))
        pl.semaphore_signal(barrier, inc=1, device_id=other, device_id_type=MESH)

    @pl.loop(1, N_LEV)
    def _(k):
        other = (lax.rem(my_lev + k, N_LEV), my_row)
        pl.semaphore_signal(barrier, inc=1, device_id=other, device_id_type=MESH)

    loads[0].wait()
    halo_send[0] = t[pl.ds(3, 512, stride=4), :]
    halo_send[1] = t[pl.ds(0, 512, stride=4), :]
    pl.semaphore_wait(barrier, N_ROW + N_LEV - 2)

    @pl.loop(1, N_ROW)
    def _(k):
        other = (my_lev, lax.rem(my_row + k, N_ROW))
        pl.semaphore_signal(ready, inc=1, device_id=other, device_id_type=MESH)


    def exchange(send, recv, rows, slot):
        c = pltpu.make_async_remote_copy(
            send.at[slot], recv.at[slot], hs_sem.at[rows + slot], hr_sem.at[rows + slot],
            device_id=(my_lev, (up_row, down_row)[slot]), device_id_type=MESH,
        )
        c.start()
        return c

    halo = [exchange(halo_send, halo_recv, 0, s) for s in (0, 1)]
    for c in loads[1:5]:
        c.wait()

    tile_row = iota((128, 128), 0)
    tile_lane = iota((128, 128), 1)
    strip_row = tile_row & 3

    def from_left(v):
        rolled = pltpu.roll(v, 1, 1)
        carried = jnp.where(tile_row < 4, 0.0, pltpu.roll(rolled, 4, 0))
        return jnp.where(tile_lane == 0, carried, rolled)

    def from_right(v):
        rolled = pltpu.roll(v, 127, 1)
        carried = jnp.where(tile_row >= 124, 0.0, pltpu.roll(rolled, 124, 0))
        return jnp.where(tile_lane == 127, carried, rolled)

    def from_before(v):
        return jnp.where(strip_row == 0, 0.0, pltpu.roll(v, 1, 0))

    def from_after(v):
        return jnp.where(strip_row == 3, 0.0, pltpu.roll(v, 127, 0))

    @pl.loop(0, 16)
    def _(lev):
        at = pl.ds(pl.multiple_of(lev * 128, 128), 128)
        v, a, b = t[at], cx[at], cy[at]
        work[at] = (
            (1.0 - a - b) * v
            + a * jnp.where(sx[at] != 0, from_before(v), from_after(v))
            + b * jnp.where(sy[at] != 0, from_left(v), from_right(v))
        )

    first = pl.ds(0, 512, stride=4)
    final = pl.ds(3, 512, stride=4)
    for c in halo:
        c.wait()
    has_down = jnp.where(my_row > 0, 1.0, 0.0)
    has_up = jnp.where(my_row < N_ROW - 1, 1.0, 0.0)
    work[first, :] = work[first, :] + has_down * jnp.where(sx[first, :] != 0, cx[first, :] * halo_recv[0], 0.0)
    work[final, :] = work[final, :] + has_up * jnp.where(sx[final, :] != 0, 0.0, cx[final, :] * halo_recv[1])

    pl.semaphore_wait(ready, N_ROW - 1)

    low = iota((8, 128), 0) < 4
    here = my_row * N_LEV + my_lev

    @pl.loop(0, 16)
    def _(k):
        pair = lax.rem(k + me // 8, 16)
        at = pl.multiple_of(pair * 8, 8)
        groups = []
        for group in range(4):
            v = [work[pl.ds(pl.multiple_of((group * 4 + g) * 128 + at, 8), 8), :] for g in range(4)]
            groups.append(swap4(v, 32))
        for half in range(2):
            for q in range(4):
                a, b = groups[half * 2][q], groups[half * 2 + 1][q]
                send_a[at + q, half * 8:half * 8 + 8] = jnp.where(low, a, pltpu.roll(b, 4, 0))
                send_a[at + 4 + q, half * 8:half * 8 + 8] = jnp.where(low, pltpu.roll(a, 4, 0), b)

        @pl.loop(0, 8)
        def _(e):
            @pl.when(k + e > 0)
            def _():
                other = at + lax.rem(e + me, 8)
                pltpu.make_async_remote_copy(
                    send_a.at[other], recv_a.at[here], as_sem, ar_sem, device_id=place(other), device_id_type=MESH
                ).start()

            @pl.when(k + e == 0)
            def _():
                pltpu.make_async_copy(send_a.at[me], recv_a.at[here], own_sem).start()

    def all_of(send, recv, ss, rs):
        return pltpu.make_async_remote_copy(
            send.at[pl.ds(0, N - 1)], recv.at[pl.ds(0, N - 1)], ss, rs,
            device_id=(my_lev, up_row), device_id_type=MESH,
        )

    loads[5].wait()
    pltpu.make_async_copy(send_a.at[me], recv_a.at[here], own_sem).wait()
    flow = all_of(send_a, recv_a, as_sem, ar_sem)
    flow.wait_recv()

    @pl.loop(0, 16, unroll=2)
    def _(j):
        v = recv_a[pl.ds(j * 8, 8)].reshape(128, 128).T
        for r, u in enumerate(swap4([v[g * 32:g * 32 + 32] for g in range(4)], 1)):
            cols[pl.ds(pl.multiple_of(j * 128 + r * 32, 32), 32), :] = u

    @pl.loop(0, 32, unroll=4)
    def _(y):
        v = dot_split(cols[pl.ds(y, 64, stride=32), :], mat[y], ((1,), (1,)))
        at = pl.ds(pl.multiple_of(y * 64, 64), 64)
        field[at] = v
        h, l = halves(v)
        parts[at, 0:128] = h
        parts[at, 128:256] = l

    final_copy = pltpu.make_async_copy(field, final_out, out_sem.at[0])
    final_copy.start()

    lanes = iota((REC_TILE, 128), 1)

    def column(ref, base):
        return jnp.concatenate([as_column(ref(base + s)) for s in range(REC_TILE // 128)], axis=0)

    def pick(base, row_of, lane_of, out):
        rows = column(row_of, base)
        for k in range(16):
            hot[:, k * 128:k * 128 + 128] = one_hot(rows == lanes + k * 128)
        g = dot(hot[...], parts[...], ((1,), (0,)))
        g = g[:, :128] + g[:, 128:]
        g = jnp.sum(jnp.where(column(lane_of, base) == lanes, g, 0.0), axis=1, keepdims=True)
        for s in range(REC_TILE // 128):
            out[pl.ds(base + s, 1), :] = as_row(g[s * 128:s * 128 + 128])

    @pl.loop(0, 4)
    def _(u):
        pick(u * 4, lambda s: rcell[pl.ds(s, 1), :] >> 7, lambda s: rcell[pl.ds(s, 1), :] & 127, picked)

    crossing = jax.nn.sigmoid(2.0 * (picked[...] - rlim[...]))
    cross_out[...] = crossing
    picked[...] = 2.0 * crossing * (1.0 - crossing)

    @pl.loop(0, 16)
    def _(u):
        seeds = as_column(picked[pl.ds(u, 1), :])
        mask = as_column(rcell[pl.ds(u, 1), :] & 127) == tile_lane
        h, l = halves(jnp.where(mask, seeds, 0.0))
        at = pl.ds(pl.multiple_of(u * 128, 128), 128)
        values[at, 0:128] = h
        values[at, 128:256] = l

    @pl.loop(0, 4)
    def _(u):
        rows = iota((REC_TILE, 128), 0) + u * REC_TILE
        for k in range(16):
            hot[:, k * 128:k * 128 + 128] = one_hot((rcell[k:k + 1, :] >> 7) == rows)
        g = dot(hot[...], values[...], ((1,), (0,)))
        work[pl.ds(pl.multiple_of(u * REC_TILE, REC_TILE), REC_TILE), :] = g[:, :128] + g[:, 128:]

    @pl.loop(0, 32, unroll=4)
    def _(y):
        at = pl.ds(pl.multiple_of(y * 64, 64), 64)
        cols[pl.ds(y, 64, stride=32), :] = dot_split(work[at], mat[y], ((1,), (0,)))

    flow.wait_send()

    @pl.loop(0, 16)
    def _(k):
        j = lax.rem(k + my_row, N_ROW)
        v = [cols[pl.ds(pl.multiple_of(j * 128 + r * 32, 32), 32), :] for r in range(4)]
        v = jnp.concatenate(swap4(v, 1), axis=0).T
        send_a[pl.ds(j * 8, 8)] = v.reshape(8, 16, 128)

        @pl.loop(0, 8)
        def _(e):
            i = lax.rem(e + my_lev, N_LEV)

            @pl.when(k + e > 0)
            def _():
                pltpu.make_async_remote_copy(
                    send_a.at[j * 8 + i], recv_b.at[me], bs_sem, br_sem, device_id=(i, j), device_id_type=MESH
                ).start()

            @pl.when(k + e == 0)
            def _():
                pltpu.make_async_copy(send_a.at[here], recv_b.at[me], own_sem).start()

    pltpu.make_async_copy(send_a.at[here], recv_b.at[me], own_sem).wait()
    flow = all_of(send_a, recv_b, bs_sem, br_sem)
    flow.wait_recv()

    @pl.loop(0, 16)
    def _(pair):
        at = pl.multiple_of(pair * 8, 8)
        for half in range(2):
            va, vb = [], []
            for q in range(4):
                p = recv_b[at + q, half * 8:half * 8 + 8]
                s = recv_b[at + 4 + q, half * 8:half * 8 + 8]
                va.append(jnp.where(low, p, pltpu.roll(s, 4, 0)))
                vb.append(jnp.where(low, pltpu.roll(p, 4, 0), s))
            for group, v in ((half * 2, va), (half * 2 + 1, vb)):
                for g, u in enumerate(swap4(v, 32)):
                    t[pl.ds(pl.multiple_of((group * 4 + g) * 128 + at, 8), 8), :] = u

    hback_send[0] = jnp.where(sx[final, :] != 0, 0.0, cx[final, :] * t[final, :])
    hback_send[1] = jnp.where(sx[first, :] != 0, cx[first, :] * t[first, :], 0.0)
    halo = [exchange(hback_send, hback_recv, 2, s) for s in (0, 1)]

    @pl.loop(0, 16)
    def _(lev):
        at = pl.ds(pl.multiple_of(lev * 128, 128), 128)
        v, a, b = t[at], cx[at], cy[at]
        flux_x, flux_y = a * v, b * v
        lower_x, lower_y = sx[at] != 0, sy[at] != 0
        work[at] = (
            (1.0 - a - b) * v
            + from_after(jnp.where(lower_x, flux_x, 0.0))
            + from_before(jnp.where(lower_x, 0.0, flux_x))
            + from_right(jnp.where(lower_y, flux_y, 0.0))
            + from_left(jnp.where(lower_y, 0.0, flux_y))
        )

    for c in halo:
        c.wait()
    work[first, :] = work[first, :] + has_down * hback_recv[0]
    work[final, :] = work[final, :] + has_up * hback_recv[1]
    adj_copy = pltpu.make_async_copy(work, adj_out, out_sem.at[1])
    adj_copy.start()

    @pl.loop(0, 16)
    def _(lev):
        at = pl.ds(pl.multiple_of(lev * 128, 128), 128)
        h, l = halves(work[at])
        parts[at, 0:128] = h
        parts[at, 128:256] = l

    def stack_row(s):
        c = scell[pl.ds(s, 1), :]
        return (c >> 14) * 128 + ((c >> 7) & 31) * 4 + ((c >> 12) & 3)

    pick(0, stack_row, lambda s: scell[pl.ds(s, 1), :] & 127, picked)
    stack_values = picked[0:4, :] * swt[...]
    partial = jnp.zeros((128, 256), F32)
    wide = iota((128, 256), 1)
    for s in range(4):
        owner = one_hot(sdest[s:s + 1, :] == tile_row)
        slot = as_column(sslot[s:s + 1, :])
        amount = as_column(stack_values[s:s + 1, :])
        slot = jnp.concatenate([slot, slot], axis=1)
        amount = jnp.concatenate([amount, amount], axis=1)
        h, l = halves(jnp.where(slot == wide, amount, 0.0))
        partial = partial + (dot(owner, h, ((1,), (0,))) + dot(owner, l, ((1,), (0,))))
    level_send[...] = partial.reshape(N_LEV, N_ROW, 256)
    level_recv[my_lev] = level_send[my_lev]

    @pl.loop(1, N_LEV)
    def _(k):
        other = lax.rem(my_lev + k, N_LEV)
        pltpu.make_async_remote_copy(
            level_send.at[other], level_recv.at[my_lev], cs_sem.at[0], cr_sem.at[0],
            device_id=(other, my_row), device_id_type=MESH,
        ).start()

    def all_but_one(send, recv, n, slot):
        return pltpu.make_async_remote_copy(
            send.at[pl.ds(0, n - 1)], recv.at[pl.ds(0, n - 1)], cs_sem.at[slot], cr_sem.at[slot],
            device_id=(my_lev, up_row), device_id_type=MESH,
        )

    levels = all_but_one(level_send, level_recv, N_LEV, 0)
    levels.wait_recv()
    total = jnp.sum(level_recv[...], axis=0)
    row_send[:, 0, :] = total[:, :128]
    row_send[:, 1, :] = total[:, 128:]
    row_recv[my_row] = row_send[my_row]

    @pl.loop(1, N_ROW)
    def _(k):
        other = lax.rem(my_row + k, N_ROW)
        pltpu.make_async_remote_copy(
            row_send.at[other], row_recv.at[my_row], cs_sem.at[1], cr_sem.at[1],
            device_id=(my_lev, other), device_id_type=MESH,
        ).start()

    last = all_but_one(row_send, row_recv, N_ROW, 1)
    last.wait_recv()
    inv_out[...] = jnp.sum(row_recv[...], axis=0)
    levels.wait_send()
    last.wait_send()
    flow.wait_send()
    final_copy.wait()
    adj_copy.wait()


def write_out(*refs):
    n = len(refs) // 2
    sems = refs[-1]
    copies = []
    for a, b in zip(refs[:n], refs[n:-1]):
        rows = a.shape[0]
        step = min(rows, 512)
        for at in range(0, rows, step):
            c = pltpu.make_async_copy(a.at[pl.ds(at, step)], b.at[pl.ds(at, step)], sems.at[len(copies)])
            c.start()
            copies.append(c)
    for c in copies:
        c.wait()


def rows_of(slab):
    return slab.reshape(16, 4, 32, 128).transpose(0, 2, 1, 3).reshape(ROWS, 128)


def local(
    tracer, courant_x, courant_y, wind_x, wind_y, inverse_diffusion,
    receptor_cell, receptor_limit, stack_cell, stack_dest, stack_slot, stack_weight,
):
    vmem = pl.BlockSpec(memory_space=pltpu.VMEM)
    hbm = pl.BlockSpec(memory_space=pl.ANY)
    slab = pltpu.VMEM((ROWS, 128), F32)
    dma = pltpu.SemaphoreType.DMA
    blocks = pltpu.VMEM((N, 16, 128), F32)
    edge = pltpu.VMEM((2, 512, 128), F32)
    results = pl.pallas_call(
        kernel,
        out_shape=(
            jax.ShapeDtypeStruct((ROWS, 128), F32),
            jax.ShapeDtypeStruct((16, 128), F32),
            jax.ShapeDtypeStruct((ROWS, 128), F32),
            jax.ShapeDtypeStruct((2, 128), F32),
        ),
        in_specs=[hbm] * 6 + [vmem] * 6,
        out_specs=(hbm, vmem, hbm, vmem),
        scratch_shapes=[
            slab, slab, slab, pltpu.VMEM((ROWS, 128), I32), pltpu.VMEM((ROWS, 128), I32), pltpu.VMEM((32, 128, 128), F32),
            slab, slab, slab, pltpu.VMEM((ROWS, 256), BF16), pltpu.VMEM((REC_TILE, ROWS), BF16),
            pltpu.VMEM((ROWS, 256), BF16), blocks, blocks, blocks,
            pltpu.VMEM((N_LEV, N_ROW, 256), F32), pltpu.VMEM((N_LEV, N_ROW, 256), F32),
            pltpu.VMEM((N_ROW, 2, 128), F32), pltpu.VMEM((N_ROW, 2, 128), F32),
            edge, edge, edge, edge, pltpu.VMEM((16, 128), F32),
            dma((6,)), dma, dma((2,)), dma((4,)), dma((4,)), dma, dma, dma, dma, dma((2,)), dma((2,)), pltpu.SemaphoreType.REGULAR,
        ],
        compiler_params=pltpu.CompilerParams(
            collective_id=0, has_side_effects=True, vmem_limit_bytes=56 * 1024 * 1024
        ),
        name="transport",
    )(
        rows_of(tracer), rows_of(courant_x), rows_of(courant_y), rows_of(wind_x), rows_of(wind_y), inverse_diffusion,
        receptor_cell.reshape(16, 128), receptor_limit.reshape(16, 128), stack_cell.reshape(4, 128),
        stack_dest.reshape(4, 128), stack_slot.reshape(4, 128), stack_weight.reshape(4, 128),
    )
    final_field, crossing, adjoint, inventory = pl.pallas_call(
        write_out,
        out_shape=tuple(jax.ShapeDtypeStruct(r.shape, r.dtype) for r in results),
        in_specs=[hbm] * 4,
        out_specs=(hbm,) * 4,
        scratch_shapes=[dma((10,))],
        name="write_out",
    )(*results)
    adjoint = adjoint.reshape(16, 32, 4, 128).transpose(0, 2, 1, 3).reshape(16, 4, 4096)
    return final_field.reshape(32, 64, 128), crossing.reshape(-1), adjoint, inventory.reshape(-1)


def solution(mesh):
    slab = P("lev", "row", None)
    flat = P(("lev", "row"))
    return jax.shard_map(
        local,
        mesh=mesh,
        in_specs=(slab,) * 5 + (P(("lev", "row"), None, None), flat, flat, flat, P(("lev", "row"), None), flat, flat),
        out_specs=(P(("lev", "row"), None, None), flat, slab, flat),
        check_vma=False,
    )
```

```python
import functools

import jax
import jax.numpy as jnp
from jax import lax
from jax.experimental import pallas as pl
from jax.experimental.pallas import tpu as pltpu
from jax.sharding import PartitionSpec as P

F32 = jnp.float32
BF16 = jnp.bfloat16
I32 = jnp.int32
MESH = pl.DeviceIdType.MESH
N_LEV = 8
N_ROW = 16
N = N_LEV * N_ROW
ROWS = 2048
REC_TILE = 512


def place(d):
    return (d // N_ROW, lax.rem(d, N_ROW))


def iota(shape, dim):
    return lax.broadcasted_iota(I32, shape, dim)


def swap4(v, unit):
    lane = iota(v[0].shape, 1)
    for bit in (1, 2):
        step = unit * bit
        high = (lane & step) != 0
        out = list(v)
        for a in range(4):
            if a & bit:
                continue
            b = a | bit
            out[a] = jnp.where(high, pltpu.roll(v[b], step, 1), v[a])
            out[b] = jnp.where(high, v[b], pltpu.roll(v[a], 128 - step, 1))
        v = out
    return v


def as_column(row):
    return jnp.broadcast_to(row, (128, 128)).T


def as_row(column):
    eye = iota((128, 128), 0) == iota((128, 128), 1)
    return jnp.sum(jnp.where(eye, jnp.broadcast_to(column, (128, 128)), 0.0), axis=0, keepdims=True)


def halves(v):
    high = v.astype(BF16)
    return high, (v - high.astype(F32)).astype(BF16)


def dot(a, b, dims):
    return lax.dot_general(a, b, (dims, ((), ())), preferred_element_type=F32)


def dot_split(a, b, dims):
    n = a.shape[0]
    side = 0 if dims[1] == (1,) else 1
    g = dot(jnp.concatenate(halves(a), axis=0), jnp.concatenate(halves(b), axis=side), dims)
    return (g[:n, :128] + g[n:, :128]) + (g[:n, 128:] + g[n:, 128:])


def one_hot(mask):
    return jnp.where(mask, 1.0, 0.0).astype(BF16)


def kernel(
    t_in, cx_in, cy_in, sx_in, sy_in, mat_in, rcell, rlim, scell, sdest, sslot, swt,
    final_out, cross_out, adj_out, inv_out,
    t, cx, cy, sx, sy, mat, work, cols, field, parts, hot, values, send_a, recv_a, recv_b, level_send, level_recv, row_send, row_recv,
    halo_send, halo_recv, hback_send, hback_recv, picked,
    load_sem, own_sem, out_sem, hs_sem, hr_sem, as_sem, ar_sem, bs_sem, br_sem, cs_sem, cr_sem, ready,
):
    my_lev = lax.axis_index("lev")
    my_row = lax.axis_index("row")
    me = my_lev * N_ROW + my_row
    up_row = lax.rem(my_row + 1, N_ROW)
    down_row = lax.rem(my_row + N_ROW - 1, N_ROW)

    loads = []
    for n, (src, dst) in enumerate(((t_in, t), (cx_in, cx), (cy_in, cy), (sx_in, sx), (sy_in, sy), (mat_in, mat))):
        c = pltpu.make_async_copy(src, dst, load_sem.at[n])
        c.start()
        loads.append(c)

    barrier = pltpu.get_barrier_semaphore()

    @pl.loop(1, N_ROW)
    def _(k):
        other = (my_lev, lax.rem(my_row + k, N_ROW))
        pl.semaphore_signal(barrier, inc=1, device_id=other, device_id_type=MESH)

    @pl.loop(1, N_LEV)
    def _(k):
        other = (lax.rem(my_lev + k, N_LEV), my_row)
        pl.semaphore_signal(barrier, inc=1, device_id=other, device_id_type=MESH)

    loads[0].wait()
    my_y = my_lev // 2
    for slot, start in ((0, 3), (1, 0)):
        edge = t[pl.ds(start, 512, stride=4), :].reshape(16, 4, 8, 128)
        for p in range(4):
            halo_send[slot, p] = edge[:, p].reshape(128, 128)
    pl.semaphore_wait(barrier, N_ROW + N_LEV - 2)

    @pl.loop(1, N_ROW)
    def _(k):
        other = (my_lev, lax.rem(my_row + k, N_ROW))
        pl.semaphore_signal(ready, inc=1, device_id=other, device_id_type=MESH)


    def exchange(send, recv, base, slot, p):
        return pltpu.make_async_remote_copy(
            send.at[slot, p], recv.at[slot, p], hs_sem.at[base + slot, p], hr_sem.at[base + slot, p],
            device_id=(my_lev, (up_row, down_row)[slot]), device_id_type=MESH,
        )

    @pl.loop(0, 4)
    def _(w):
        for slot in range(2):
            exchange(halo_send, halo_recv, 0, slot, lax.rem(my_y + w, 4)).start()

    for c in loads[1:5]:
        c.wait()

    tile_row = iota((128, 128), 0)
    tile_lane = iota((128, 128), 1)
    strip_row = tile_row & 3

    def from_left(v):
        rolled = pltpu.roll(v, 1, 1)
        carried = jnp.where(tile_row < 4, 0.0, pltpu.roll(rolled, 4, 0))
        return jnp.where(tile_lane == 0, carried, rolled)

    def from_right(v):
        rolled = pltpu.roll(v, 127, 1)
        carried = jnp.where(tile_row >= 124, 0.0, pltpu.roll(rolled, 124, 0))
        return jnp.where(tile_lane == 127, carried, rolled)

    def from_before(v):
        return jnp.where(strip_row == 0, 0.0, pltpu.roll(v, 1, 0))

    def from_after(v):
        return jnp.where(strip_row == 3, 0.0, pltpu.roll(v, 127, 0))

    @pl.loop(0, 16)
    def _(lev):
        at = pl.ds(pl.multiple_of(lev * 128, 128), 128)
        v, a, b = t[at], cx[at], cy[at]
        work[at] = (
            (1.0 - a - b) * v
            + a * jnp.where(sx[at] != 0, from_before(v), from_after(v))
            + b * jnp.where(sy[at] != 0, from_left(v), from_right(v))
        )

    has_down = jnp.where(my_row > 0, 1.0, 0.0)
    has_up = jnp.where(my_row < N_ROW - 1, 1.0, 0.0)

    def edge_rows(lev, p, r):
        return pl.ds(lev * 128 + p * 32 + r, 8, stride=4)

    pl.semaphore_wait(ready, N_ROW - 1)

    low = iota((8, 128), 0) < 4
    here = my_row * N_LEV + my_lev

    @pl.loop(0, 4)
    def _(w):
        p = lax.rem(my_y + w, 4)
        for slot in range(2):
            exchange(halo_send, halo_recv, 0, slot, p).wait()
        for lev in range(16):
            e = edge_rows(lev, p, 0)
            v = cx[e, :] * halo_recv[0, p, lev * 8:lev * 8 + 8]
            work[e, :] = work[e, :] + has_down * jnp.where(sx[e, :] != 0, v, 0.0)
            e = edge_rows(lev, p, 3)
            v = cx[e, :] * halo_recv[1, p, lev * 8:lev * 8 + 8]
            work[e, :] = work[e, :] + has_up * jnp.where(sx[e, :] != 0, 0.0, v)

        @pl.loop(0, 4)
        def _(k):
            pair = p * 4 + lax.rem(k + me // 8, 4)
            at = pl.multiple_of(pair * 8, 8)
            groups = []
            for group in range(4):
                v = [work[pl.ds(pl.multiple_of((group * 4 + g) * 128 + at, 8), 8), :] for g in range(4)]
                groups.append(swap4(v, 32))
            for half in range(2):
                for q in range(4):
                    a, b = groups[half * 2][q], groups[half * 2 + 1][q]
                    send_a[at + q, half * 8:half * 8 + 8] = jnp.where(low, a, pltpu.roll(b, 4, 0))
                    send_a[at + 4 + q, half * 8:half * 8 + 8] = jnp.where(low, pltpu.roll(a, 4, 0), b)

            @pl.loop(0, 8)
            def _(e):
                @pl.when(w + k + e > 0)
                def _():
                    other = at + lax.rem(e + me, 8)
                    pltpu.make_async_remote_copy(
                        send_a.at[other], recv_a.at[here], as_sem, ar_sem, device_id=place(other), device_id_type=MESH
                    ).start()

                @pl.when(w + k + e == 0)
                def _():
                    pltpu.make_async_copy(send_a.at[me], recv_a.at[here], own_sem).start()

    def all_of(send, recv, ss, rs):
        return pltpu.make_async_remote_copy(
            send.at[pl.ds(0, N - 1)], recv.at[pl.ds(0, N - 1)], ss, rs,
            device_id=(my_lev, up_row), device_id_type=MESH,
        )

    loads[5].wait()
    pltpu.make_async_copy(send_a.at[me], recv_a.at[here], own_sem).wait()
    flow = all_of(send_a, recv_a, as_sem, ar_sem)
    flow.wait_recv()

    @pl.loop(0, 16, unroll=2)
    def _(j):
        v = recv_a[pl.ds(j * 8, 8)].reshape(128, 128).T
        for r, u in enumerate(swap4([v[g * 32:g * 32 + 32] for g in range(4)], 1)):
            cols[pl.ds(pl.multiple_of(j * 128 + r * 32, 32), 32), :] = u

    @pl.loop(0, 32, unroll=4)
    def _(y):
        v = dot_split(cols[pl.ds(y, 64, stride=32), :], mat[y], ((1,), (1,)))
        at = pl.ds(pl.multiple_of(y * 64, 64), 64)
        field[at] = v
        h, l = halves(v)
        parts[at, 0:128] = h
        parts[at, 128:256] = l

    final_copy = pltpu.make_async_copy(field, final_out, out_sem.at[0])
    final_copy.start()

    lanes = iota((REC_TILE, 128), 1)

    def column(ref, base):
        return jnp.concatenate([as_column(ref(base + s)) for s in range(REC_TILE // 128)], axis=0)

    def pick(base, row_of, lane_of, out):
        rows = column(row_of, base)
        for k in range(16):
            hot[:, k * 128:k * 128 + 128] = one_hot(rows == lanes + k * 128)
        g = dot(hot[...], parts[...], ((1,), (0,)))
        g = g[:, :128] + g[:, 128:]
        g = jnp.sum(jnp.where(column(lane_of, base) == lanes, g, 0.0), axis=1, keepdims=True)
        for s in range(REC_TILE // 128):
            out[pl.ds(base + s, 1), :] = as_row(g[s * 128:s * 128 + 128])

    @pl.loop(0, 4)
    def _(u):
        pick(u * 4, lambda s: rcell[pl.ds(s, 1), :] >> 7, lambda s: rcell[pl.ds(s, 1), :] & 127, picked)

    crossing = jax.nn.sigmoid(2.0 * (picked[...] - rlim[...]))
    cross_out[...] = crossing
    picked[...] = 2.0 * crossing * (1.0 - crossing)

    @pl.loop(0, 16)
    def _(u):
        seeds = as_column(picked[pl.ds(u, 1), :])
        mask = as_column(rcell[pl.ds(u, 1), :] & 127) == tile_lane
        h, l = halves(jnp.where(mask, seeds, 0.0))
        at = pl.ds(pl.multiple_of(u * 128, 128), 128)
        values[at, 0:128] = h
        values[at, 128:256] = l

    @pl.loop(0, 4)
    def _(u):
        rows = iota((REC_TILE, 128), 0) + u * REC_TILE
        for k in range(16):
            hot[:, k * 128:k * 128 + 128] = one_hot((rcell[k:k + 1, :] >> 7) == rows)
        g = dot(hot[...], values[...], ((1,), (0,)))
        work[pl.ds(pl.multiple_of(u * REC_TILE, REC_TILE), REC_TILE), :] = g[:, :128] + g[:, 128:]

    @pl.loop(0, 32, unroll=4)
    def _(y):
        at = pl.ds(pl.multiple_of(y * 64, 64), 64)
        cols[pl.ds(y, 64, stride=32), :] = dot_split(work[at], mat[y], ((1,), (0,)))

    flow.wait_send()

    def send_back(w, j, core):
        i = 2 * lax.rem(my_y + w, 4) + core
        block = j * N_LEV + i
        at_home = (i == my_lev) & (j == my_row)

        @pl.when(jnp.logical_not(at_home))
        def _():
            pltpu.make_async_remote_copy(
                send_a.at[block], recv_b.at[me], bs_sem.at[w], br_sem.at[w], device_id=(i, j), device_id_type=MESH
            ).start()

        @pl.when(at_home)
        def _():
            pltpu.make_async_copy(send_a.at[here], recv_b.at[me], own_sem).start()

    @pl.loop(0, 16)
    def _(k):
        j = lax.rem(5 * k + my_row, N_ROW)
        v = [cols[pl.ds(pl.multiple_of(j * 128 + r * 32, 32), 32), :] for r in range(4)]
        v = jnp.concatenate(swap4(v, 1), axis=0).T
        send_a[pl.ds(j * 8, 8)] = v.reshape(8, 16, 128)

        for core in range(2):
            send_back(0, j, core)

    @pl.loop(1, 4)
    def _(w):
        @pl.loop(0, 16)
        def _(k):
            for core in range(2):
                send_back(w, lax.rem(5 * k + my_row, N_ROW), core)

    def wave(w, n):
        return pltpu.make_async_remote_copy(
            send_a.at[pl.ds(0, n)], recv_b.at[pl.ds(0, n)], bs_sem.at[w], br_sem.at[w],
            device_id=(my_lev, up_row), device_id_type=MESH,
        )

    pltpu.make_async_copy(send_a.at[here], recv_b.at[me], own_sem).wait()
    for w in range(4):
        wave(w, 31 if w == 0 else 32).wait_recv()
        p = lax.rem(my_y + 4 - w, 4)

        @pl.loop(0, 4)
        def _(k):
            at = pl.multiple_of((p * 4 + k) * 8, 8)
            for half in range(2):
                va, vb = [], []
                for q in range(4):
                    u = recv_b[at + q, half * 8:half * 8 + 8]
                    s = recv_b[at + 4 + q, half * 8:half * 8 + 8]
                    va.append(jnp.where(low, u, pltpu.roll(s, 4, 0)))
                    vb.append(jnp.where(low, pltpu.roll(u, 4, 0), s))
                for group, v in ((half * 2, va), (half * 2 + 1, vb)):
                    for g, u in enumerate(swap4(v, 32)):
                        t[pl.ds(pl.multiple_of((group * 4 + g) * 128 + at, 8), 8), :] = u

        for lev in range(16):
            e = edge_rows(lev, p, 3)
            hback_send[0, p, lev * 8:lev * 8 + 8] = jnp.where(sx[e, :] != 0, 0.0, cx[e, :] * t[e, :])
            e = edge_rows(lev, p, 0)
            hback_send[1, p, lev * 8:lev * 8 + 8] = jnp.where(sx[e, :] != 0, cx[e, :] * t[e, :], 0.0)
        for slot in range(2):
            exchange(hback_send, hback_recv, 2, slot, p).start()

    @pl.loop(0, 16)
    def _(lev):
        at = pl.ds(pl.multiple_of(lev * 128, 128), 128)
        v, a, b = t[at], cx[at], cy[at]
        flux_x, flux_y = a * v, b * v
        lower_x, lower_y = sx[at] != 0, sy[at] != 0
        work[at] = (
            (1.0 - a - b) * v
            + from_after(jnp.where(lower_x, flux_x, 0.0))
            + from_before(jnp.where(lower_x, 0.0, flux_x))
            + from_right(jnp.where(lower_y, flux_y, 0.0))
            + from_left(jnp.where(lower_y, 0.0, flux_y))
        )

    for p in range(4):
        for slot in range(2):
            exchange(hback_send, hback_recv, 2, slot, p).wait()

    def edge_of(slot):
        return jnp.concatenate(
            [hback_recv[slot, p, lev * 8:lev * 8 + 8] for lev in range(16) for p in range(4)], axis=0
        )

    first = pl.ds(0, 512, stride=4)
    final = pl.ds(3, 512, stride=4)
    work[first, :] = work[first, :] + has_down * edge_of(0)
    work[final, :] = work[final, :] + has_up * edge_of(1)
    adj_copy = pltpu.make_async_copy(work, adj_out, out_sem.at[1])
    adj_copy.start()

    @pl.loop(0, 16)
    def _(lev):
        at = pl.ds(pl.multiple_of(lev * 128, 128), 128)
        h, l = halves(work[at])
        parts[at, 0:128] = h
        parts[at, 128:256] = l

    def stack_row(s):
        c = scell[pl.ds(s, 1), :]
        return (c >> 14) * 128 + ((c >> 7) & 31) * 4 + ((c >> 12) & 3)

    pick(0, stack_row, lambda s: scell[pl.ds(s, 1), :] & 127, picked)
    stack_values = picked[0:4, :] * swt[...]
    partial = jnp.zeros((128, 256), F32)
    wide = iota((128, 256), 1)
    for s in range(4):
        owner = one_hot(sdest[s:s + 1, :] == tile_row)
        slot = as_column(sslot[s:s + 1, :])
        amount = as_column(stack_values[s:s + 1, :])
        slot = jnp.concatenate([slot, slot], axis=1)
        amount = jnp.concatenate([amount, amount], axis=1)
        h, l = halves(jnp.where(slot == wide, amount, 0.0))
        partial = partial + (dot(owner, h, ((1,), (0,))) + dot(owner, l, ((1,), (0,))))
    level_send[...] = partial.reshape(N_LEV, N_ROW, 256)
    level_recv[my_lev] = level_send[my_lev]

    @pl.loop(1, N_LEV)
    def _(k):
        other = lax.rem(my_lev + k, N_LEV)
        pltpu.make_async_remote_copy(
            level_send.at[other], level_recv.at[my_lev], cs_sem.at[0], cr_sem.at[0],
            device_id=(other, my_row), device_id_type=MESH,
        ).start()

    def all_but_one(send, recv, n, slot):
        return pltpu.make_async_remote_copy(
            send.at[pl.ds(0, n - 1)], recv.at[pl.ds(0, n - 1)], cs_sem.at[slot], cr_sem.at[slot],
            device_id=(my_lev, up_row), device_id_type=MESH,
        )

    levels = all_but_one(level_send, level_recv, N_LEV, 0)
    levels.wait_recv()
    total = jnp.sum(level_recv[...], axis=0)
    row_send[:, 0, :] = total[:, :128]
    row_send[:, 1, :] = total[:, 128:]
    row_recv[my_row] = row_send[my_row]

    @pl.loop(1, N_ROW)
    def _(k):
        other = lax.rem(my_row + k, N_ROW)
        pltpu.make_async_remote_copy(
            row_send.at[other], row_recv.at[my_row], cs_sem.at[1], cr_sem.at[1],
            device_id=(my_lev, other), device_id_type=MESH,
        ).start()

    last = all_but_one(row_send, row_recv, N_ROW, 1)
    last.wait_recv()
    inv_out[...] = jnp.sum(row_recv[...], axis=0)
    levels.wait_send()
    last.wait_send()
    for w in range(4):
        wave(w, 31 if w == 0 else 32).wait_send()
    final_copy.wait()
    adj_copy.wait()


def write_out(*refs):
    stages = [], []
    for a, b, held in zip(refs[:4], refs[4:8], refs[8:12]):
        rows = a.shape[0]
        step = min(rows, 512)
        for at in range(0, rows, step):
            for n, (src, dst) in enumerate(((a, held), (held, b))):
                here = pl.ds(at, step)
                stages[n].append(pltpu.make_async_copy(src.at[here], dst.at[here], refs[12].at[n, len(stages[n])]))
    for c in stages[0]:
        c.start()
    for c, d in zip(*stages):
        c.wait()
        d.start()
    for d in stages[1]:
        d.wait()


def rows_of(slab):
    return slab.reshape(16, 4, 32, 128).transpose(0, 2, 1, 3).reshape(ROWS, 128)


def local(
    tracer, courant_x, courant_y, wind_x, wind_y, inverse_diffusion,
    receptor_cell, receptor_limit, stack_cell, stack_dest, stack_slot, stack_weight,
):
    vmem = pl.BlockSpec(memory_space=pltpu.VMEM)
    hbm = pl.BlockSpec(memory_space=pl.ANY)
    slab = pltpu.VMEM((ROWS, 128), F32)
    dma = pltpu.SemaphoreType.DMA
    blocks = pltpu.VMEM((N, 16, 128), F32)
    edge = pltpu.VMEM((2, 4, 128, 128), F32)
    results = pl.pallas_call(
        kernel,
        out_shape=(
            jax.ShapeDtypeStruct((ROWS, 128), F32),
            jax.ShapeDtypeStruct((16, 128), F32),
            jax.ShapeDtypeStruct((ROWS, 128), F32),
            jax.ShapeDtypeStruct((2, 128), F32),
        ),
        in_specs=[hbm] * 6 + [vmem] * 6,
        out_specs=(hbm, vmem, hbm, vmem),
        scratch_shapes=[
            slab, slab, slab, pltpu.VMEM((ROWS, 128), I32), pltpu.VMEM((ROWS, 128), I32), pltpu.VMEM((32, 128, 128), F32),
            slab, slab, slab, pltpu.VMEM((ROWS, 256), BF16), pltpu.VMEM((REC_TILE, ROWS), BF16),
            pltpu.VMEM((ROWS, 256), BF16), blocks, blocks, blocks,
            pltpu.VMEM((N_LEV, N_ROW, 256), F32), pltpu.VMEM((N_LEV, N_ROW, 256), F32),
            pltpu.VMEM((N_ROW, 2, 128), F32), pltpu.VMEM((N_ROW, 2, 128), F32),
            edge, edge, edge, edge, pltpu.VMEM((16, 128), F32),
            dma((6,)), dma, dma((2,)), dma((4, 4)), dma((4, 4)), dma, dma, dma((4,)), dma((4,)), dma((2,)), dma((2,)), pltpu.SemaphoreType.REGULAR,
        ],
        compiler_params=pltpu.CompilerParams(
            collective_id=0, has_side_effects=True, vmem_limit_bytes=56 * 1024 * 1024
        ),
        name="transport",
    )(
        rows_of(tracer), rows_of(courant_x), rows_of(courant_y), rows_of(wind_x), rows_of(wind_y), inverse_diffusion,
        receptor_cell.reshape(16, 128), receptor_limit.reshape(16, 128), stack_cell.reshape(4, 128),
        stack_dest.reshape(4, 128), stack_slot.reshape(4, 128), stack_weight.reshape(4, 128),
    )
    final_field, crossing, adjoint, inventory = pl.pallas_call(
        write_out,
        out_shape=tuple(jax.ShapeDtypeStruct(r.shape, r.dtype) for r in results),
        in_specs=[hbm] * 4,
        out_specs=(hbm,) * 4,
        scratch_shapes=[pltpu.VMEM(r.shape, r.dtype) for r in results] + [dma((2, 10))],
        name="write_out",
    )(*results)
    adjoint = adjoint.reshape(16, 32, 4, 128).transpose(0, 2, 1, 3).reshape(16, 4, 4096)
    return final_field.reshape(32, 64, 128), crossing.reshape(-1), adjoint, inventory.reshape(-1)


def solution(mesh):
    slab = P("lev", "row", None)
    flat = P(("lev", "row"))
    return jax.shard_map(
        local,
        mesh=mesh,
        in_specs=(slab,) * 5 + (P(("lev", "row"), None, None), flat, flat, flat, P(("lev", "row"), None), flat, flat),
        out_specs=(P(("lev", "row"), None, None), flat, slab, flat),
        check_vma=False,
    )
```

```python
import functools

import jax
import jax.numpy as jnp
from jax import lax
from jax.experimental import pallas as pl
from jax.experimental.pallas import tpu as pltpu
from jax.sharding import PartitionSpec as P

F32 = jnp.float32
BF16 = jnp.bfloat16
I32 = jnp.int32
MESH = pl.DeviceIdType.MESH
N_LEV = 8
N_ROW = 16
N = N_LEV * N_ROW
ROWS = 2048
TILE = 1024


def place(d):
    return (d // N_ROW, lax.rem(d, N_ROW))


def iota(shape, dim):
    return lax.broadcasted_iota(I32, shape, dim)


def swap4(v, unit):
    lane = iota(v[0].shape, 1)
    for bit in (1, 2):
        step = unit * bit
        high = (lane & step) != 0
        out = list(v)
        for a in range(4):
            if a & bit:
                continue
            b = a | bit
            out[a] = jnp.where(high, pltpu.roll(v[b], step, 1), v[a])
            out[b] = jnp.where(high, v[b], pltpu.roll(v[a], 128 - step, 1))
        v = out
    return v


def as_column(row):
    return jnp.broadcast_to(row, (128, 128)).T


def as_row(column):
    eye = iota((128, 128), 0) == iota((128, 128), 1)
    return jnp.sum(jnp.where(eye, jnp.broadcast_to(column, (128, 128)), 0.0), axis=0, keepdims=True)


def halves(v):
    high = v.astype(BF16)
    return high, (v - high.astype(F32)).astype(BF16)


def dot(a, b, dims):
    return lax.dot_general(a, b, (dims, ((), ())), preferred_element_type=F32)


def dot_split(a, b, dims):
    n = a.shape[0]
    side = 0 if dims[1] == (1,) else 1
    g = dot(jnp.concatenate(halves(a), axis=0), jnp.concatenate(halves(b), axis=side), dims)
    return (g[:n, :128] + g[n:, :128]) + (g[:n, 128:] + g[n:, 128:])


def one_hot(mask):
    return jnp.where(mask, 1.0, 0.0).astype(BF16)


def kernel(
    t_in, cx_in, cy_in, sx_in, sy_in, mat_in, rcell_in, rlim_in, scell_in, sdest_in, sslot_in, swt_in,
    final_out, cross_out, adj_out, inv_out,
    t, cx, cy, sx, sy, mat, rcell, rlim, scell, sdest, sslot, swt, cross, inv, work, cols, field, parts, values, send_a, recv_a, recv_b, level_send, level_recv, row_send, row_recv,
    halo_send, halo_recv, hback_send, hback_recv, picked,
    load_sem, own_sem, out_sem, hs_sem, hr_sem, as_sem, ar_sem, bs_sem, br_sem, cs_sem, cr_sem, ready,
):
    my_lev = lax.axis_index("lev")
    my_row = lax.axis_index("row")
    me = my_lev * N_ROW + my_row
    up_row = lax.rem(my_row + 1, N_ROW)
    down_row = lax.rem(my_row + N_ROW - 1, N_ROW)

    loads = []
    inputs = (
        (t_in, t), (cx_in, cx), (cy_in, cy), (sx_in, sx), (sy_in, sy), (mat_in, mat), (rcell_in, rcell),
        (rlim_in, rlim), (scell_in, scell), (sdest_in, sdest), (sslot_in, sslot), (swt_in, swt),
    )
    for n, (src, dst) in enumerate(inputs):
        c = pltpu.make_async_copy(src, dst, load_sem.at[n])
        c.start()
        loads.append(c)

    barrier = pltpu.get_barrier_semaphore()

    @pl.loop(1, N_ROW)
    def _(k):
        other = (my_lev, lax.rem(my_row + k, N_ROW))
        pl.semaphore_signal(barrier, inc=1, device_id=other, device_id_type=MESH)

    @pl.loop(1, N_LEV)
    def _(k):
        other = (lax.rem(my_lev + k, N_LEV), my_row)
        pl.semaphore_signal(barrier, inc=1, device_id=other, device_id_type=MESH)

    loads[0].wait()
    my_y = my_lev // 2
    for slot, start in ((0, 3), (1, 0)):
        edge = t[pl.ds(start, 512, stride=4), :].reshape(16, 4, 8, 128)
        for p in range(4):
            halo_send[slot, p] = edge[:, p].reshape(128, 128)
    pl.semaphore_wait(barrier, N_ROW + N_LEV - 2)

    @pl.loop(1, N_ROW)
    def _(k):
        other = (my_lev, lax.rem(my_row + k, N_ROW))
        pl.semaphore_signal(ready, inc=1, device_id=other, device_id_type=MESH)


    def exchange(send, recv, base, slot, p):
        return pltpu.make_async_remote_copy(
            send.at[slot, p], recv.at[slot, p], hs_sem.at[base + slot, p], hr_sem.at[base + slot, p],
            device_id=(my_lev, (up_row, down_row)[slot]), device_id_type=MESH,
        )

    @pl.loop(0, 4)
    def _(w):
        for slot in range(2):
            exchange(halo_send, halo_recv, 0, slot, lax.rem(my_y + w, 4)).start()

    for c in loads[1:5]:
        c.wait()

    tile_row = iota((128, 128), 0)
    tile_lane = iota((128, 128), 1)
    strip_row = tile_row & 3

    def from_left(v):
        rolled = pltpu.roll(v, 1, 1)
        carried = jnp.where(tile_row < 4, 0.0, pltpu.roll(rolled, 4, 0))
        return jnp.where(tile_lane == 0, carried, rolled)

    def from_right(v):
        rolled = pltpu.roll(v, 127, 1)
        carried = jnp.where(tile_row >= 124, 0.0, pltpu.roll(rolled, 124, 0))
        return jnp.where(tile_lane == 127, carried, rolled)

    def from_before(v):
        return jnp.where(strip_row == 0, 0.0, pltpu.roll(v, 1, 0))

    def from_after(v):
        return jnp.where(strip_row == 3, 0.0, pltpu.roll(v, 127, 0))

    @pl.loop(0, 16)
    def _(lev):
        at = pl.ds(pl.multiple_of(lev * 128, 128), 128)
        v, a, b = t[at], cx[at], cy[at]
        work[at] = (
            (1.0 - a - b) * v
            + a * jnp.where(sx[at] != 0, from_before(v), from_after(v))
            + b * jnp.where(sy[at] != 0, from_left(v), from_right(v))
        )

    has_down = jnp.where(my_row > 0, 1.0, 0.0)
    has_up = jnp.where(my_row < N_ROW - 1, 1.0, 0.0)

    def edge_rows(lev, p, r):
        return pl.ds(lev * 128 + p * 32 + r, 8, stride=4)

    pl.semaphore_wait(ready, N_ROW - 1)

    low = iota((8, 128), 0) < 4
    here = my_row * N_LEV + my_lev

    @pl.loop(0, 4)
    def _(w):
        p = lax.rem(my_y + w, 4)
        for slot in range(2):
            exchange(halo_send, halo_recv, 0, slot, p).wait()
        for lev in range(16):
            e = edge_rows(lev, p, 0)
            v = cx[e, :] * halo_recv[0, p, lev * 8:lev * 8 + 8]
            work[e, :] = work[e, :] + has_down * jnp.where(sx[e, :] != 0, v, 0.0)
            e = edge_rows(lev, p, 3)
            v = cx[e, :] * halo_recv[1, p, lev * 8:lev * 8 + 8]
            work[e, :] = work[e, :] + has_up * jnp.where(sx[e, :] != 0, 0.0, v)

        @pl.loop(0, 4)
        def _(k):
            pair = p * 4 + lax.rem(k + me // 8, 4)
            at = pl.multiple_of(pair * 8, 8)
            groups = []
            for group in range(4):
                v = [work[pl.ds(pl.multiple_of((group * 4 + g) * 128 + at, 8), 8), :] for g in range(4)]
                groups.append(swap4(v, 32))
            for half in range(2):
                for q in range(4):
                    a, b = groups[half * 2][q], groups[half * 2 + 1][q]
                    send_a[at + q, half * 8:half * 8 + 8] = jnp.where(low, a, pltpu.roll(b, 4, 0))
                    send_a[at + 4 + q, half * 8:half * 8 + 8] = jnp.where(low, pltpu.roll(a, 4, 0), b)

            @pl.loop(0, 8)
            def _(e):
                @pl.when(w + k + e > 0)
                def _():
                    other = at + lax.rem(e + me, 8)
                    pltpu.make_async_remote_copy(
                        send_a.at[other], recv_a.at[here], as_sem, ar_sem, device_id=place(other), device_id_type=MESH
                    ).start()

                @pl.when(w + k + e == 0)
                def _():
                    pltpu.make_async_copy(send_a.at[me], recv_a.at[here], own_sem).start()

    def all_of(send, recv, ss, rs):
        return pltpu.make_async_remote_copy(
            send.at[pl.ds(0, N - 1)], recv.at[pl.ds(0, N - 1)], ss, rs,
            device_id=(my_lev, up_row), device_id_type=MESH,
        )

    for c in loads[5:]:
        c.wait()
    pltpu.make_async_copy(send_a.at[me], recv_a.at[here], own_sem).wait()
    flow = all_of(send_a, recv_a, as_sem, ar_sem)
    flow.wait_recv()

    @pl.loop(0, 16, unroll=2)
    def _(j):
        v = recv_a[pl.ds(j * 8, 8)].reshape(128, 128).T
        for r, u in enumerate(swap4([v[g * 32:g * 32 + 32] for g in range(4)], 1)):
            cols[pl.ds(pl.multiple_of(j * 128 + r * 32, 32), 32), :] = u

    @pl.loop(0, 32, unroll=4)
    def _(y):
        v = dot_split(cols[pl.ds(y, 64, stride=32), :], mat[y], ((1,), (1,)))
        at = pl.ds(pl.multiple_of(y * 64, 64), 64)
        field[at] = v
        h, l = halves(v)
        parts[at, 0:128] = h
        parts[at, 128:256] = l

    final_copy = pltpu.make_async_copy(field, final_out, out_sem.at[0])
    final_copy.start()

    def column(ref, base, tile):
        return jnp.concatenate([as_column(ref(base + s)) for s in range(tile // 128)], axis=0)

    def pick(base, tile, row_of, lane_of, out):
        lanes = iota((tile, 128), 1)
        rows = column(row_of, base, tile)
        g = jnp.zeros((tile, 256), F32)
        for k in range(8):
            h = jnp.concatenate([one_hot(rows == lanes + (k * 256 + half)) for half in (0, 128)], axis=1)
            g = g + dot(h, parts[k * 256:k * 256 + 256], ((1,), (0,)))
        mask = column(lane_of, base, tile) == lanes
        g = jnp.sum(jnp.where(mask, g[:, :128] + g[:, 128:], 0.0), axis=1, keepdims=True)
        for s in range(tile // 128):
            out[pl.ds(base + s, 1), :] = as_row(g[s * 128:s * 128 + 128])
        return mask

    @pl.loop(0, 2)
    def _(u):
        mask = pick(u * 8, TILE, lambda s: rcell[pl.ds(s, 1), :] >> 7, lambda s: rcell[pl.ds(s, 1), :] & 127, picked)
        work[pl.ds(pl.multiple_of(u * TILE, TILE), TILE), :] = jnp.where(mask, 1.0, 0.0)

    crossing = jax.nn.sigmoid(2.0 * (picked[...] - rlim[...]))
    cross[...] = crossing
    cross_copy = pltpu.make_async_copy(cross, cross_out, out_sem.at[2])
    cross_copy.start()
    picked[...] = 2.0 * crossing * (1.0 - crossing)

    @pl.loop(0, 16, unroll=2)
    def _(u):
        at = pl.ds(pl.multiple_of(u * 128, 128), 128)
        h, l = halves(work[at] * as_column(picked[pl.ds(u, 1), :]))
        values[at, 0:128] = h
        values[at, 128:256] = l

    @pl.loop(0, 2)
    def _(u):
        rows = iota((TILE, 128), 0) + u * TILE
        g = jnp.zeros((TILE, 256), F32)
        for k in range(8):
            h = jnp.concatenate([one_hot((rcell[2 * k + n:2 * k + n + 1, :] >> 7) == rows) for n in (0, 1)], axis=1)
            g = g + dot(h, values[k * 256:k * 256 + 256], ((1,), (0,)))
        work[pl.ds(pl.multiple_of(u * TILE, TILE), TILE), :] = g[:, :128] + g[:, 128:]

    @pl.loop(0, 32, unroll=4)
    def _(y):
        at = pl.ds(pl.multiple_of(y * 64, 64), 64)
        cols[pl.ds(y, 64, stride=32), :] = dot_split(work[at], mat[y], ((1,), (0,)))

    flow.wait_send()

    def send_back(w, j, core):
        i = 2 * lax.rem(my_y + w, 4) + core
        block = j * N_LEV + i
        at_home = (i == my_lev) & (j == my_row)

        @pl.when(jnp.logical_not(at_home))
        def _():
            pltpu.make_async_remote_copy(
                send_a.at[block], recv_b.at[me], bs_sem.at[w], br_sem.at[w], device_id=(i, j), device_id_type=MESH
            ).start()

        @pl.when(at_home)
        def _():
            pltpu.make_async_copy(send_a.at[here], recv_b.at[me], own_sem).start()

    @pl.loop(0, 16)
    def _(k):
        j = lax.rem(5 * k + my_row, N_ROW)
        v = [cols[pl.ds(pl.multiple_of(j * 128 + r * 32, 32), 32), :] for r in range(4)]
        v = jnp.concatenate(swap4(v, 1), axis=0).T
        send_a[pl.ds(j * 8, 8)] = v.reshape(8, 16, 128)

        for core in range(2):
            send_back(0, j, core)

    def wave(w, n):
        return pltpu.make_async_remote_copy(
            send_a.at[pl.ds(0, n)], recv_b.at[pl.ds(0, n)], bs_sem.at[w], br_sem.at[w],
            device_id=(my_lev, up_row), device_id_type=MESH,
        )

    pltpu.make_async_copy(send_a.at[here], recv_b.at[me], own_sem).wait()
    for w in range(4):
        if w < 3:

            @pl.loop(0, 16)
            def _(k):
                for core in range(2):
                    send_back(w + 1, lax.rem(5 * k + my_row, N_ROW), core)

        wave(w, 31 if w == 0 else 32).wait_recv()
        p = lax.rem(my_y + 4 - w, 4)

        @pl.loop(0, 4)
        def _(k):
            at = pl.multiple_of((p * 4 + k) * 8, 8)
            for half in range(2):
                va, vb = [], []
                for q in range(4):
                    u = recv_b[at + q, half * 8:half * 8 + 8]
                    s = recv_b[at + 4 + q, half * 8:half * 8 + 8]
                    va.append(jnp.where(low, u, pltpu.roll(s, 4, 0)))
                    vb.append(jnp.where(low, pltpu.roll(u, 4, 0), s))
                for group, v in ((half * 2, va), (half * 2 + 1, vb)):
                    for g, u in enumerate(swap4(v, 32)):
                        t[pl.ds(pl.multiple_of((group * 4 + g) * 128 + at, 8), 8), :] = u

        for lev in range(16):
            e = edge_rows(lev, p, 3)
            hback_send[0, p, lev * 8:lev * 8 + 8] = jnp.where(sx[e, :] != 0, 0.0, cx[e, :] * t[e, :])
            e = edge_rows(lev, p, 0)
            hback_send[1, p, lev * 8:lev * 8 + 8] = jnp.where(sx[e, :] != 0, cx[e, :] * t[e, :], 0.0)
        for slot in range(2):
            exchange(hback_send, hback_recv, 2, slot, p).start()

    @pl.loop(0, 16)
    def _(lev):
        at = pl.ds(pl.multiple_of(lev * 128, 128), 128)
        v, a, b = t[at], cx[at], cy[at]
        flux_x, flux_y = a * v, b * v
        lower_x, lower_y = sx[at] != 0, sy[at] != 0
        work[at] = (
            (1.0 - a - b) * v
            + from_after(jnp.where(lower_x, flux_x, 0.0))
            + from_before(jnp.where(lower_x, 0.0, flux_x))
            + from_right(jnp.where(lower_y, flux_y, 0.0))
            + from_left(jnp.where(lower_y, 0.0, flux_y))
        )

    for p in range(4):
        for slot in range(2):
            exchange(hback_send, hback_recv, 2, slot, p).wait()

    def edge_of(slot):
        return jnp.concatenate(
            [hback_recv[slot, p, lev * 8:lev * 8 + 8] for lev in range(16) for p in range(4)], axis=0
        )

    first = pl.ds(0, 512, stride=4)
    final = pl.ds(3, 512, stride=4)
    work[first, :] = work[first, :] + has_down * edge_of(0)
    work[final, :] = work[final, :] + has_up * edge_of(1)
    adj_copy = pltpu.make_async_copy(work, adj_out, out_sem.at[1])
    adj_copy.start()

    @pl.loop(0, 16)
    def _(lev):
        at = pl.ds(pl.multiple_of(lev * 128, 128), 128)
        h, l = halves(work[at])
        parts[at, 0:128] = h
        parts[at, 128:256] = l

    def stack_row(s):
        c = scell[pl.ds(s, 1), :]
        return (c >> 14) * 128 + ((c >> 7) & 31) * 4 + ((c >> 12) & 3)

    pick(0, 512, stack_row, lambda s: scell[pl.ds(s, 1), :] & 127, picked)
    stack_values = picked[0:4, :] * swt[...]
    partial = jnp.zeros((128, 256), F32)
    wide = iota((128, 256), 1)
    for s in range(4):
        owner = one_hot(sdest[s:s + 1, :] == tile_row)
        slot = as_column(sslot[s:s + 1, :])
        amount = as_column(stack_values[s:s + 1, :])
        slot = jnp.concatenate([slot, slot], axis=1)
        amount = jnp.concatenate([amount, amount], axis=1)
        h, l = halves(jnp.where(slot == wide, amount, 0.0))
        partial = partial + (dot(owner, h, ((1,), (0,))) + dot(owner, l, ((1,), (0,))))
    level_send[...] = partial.reshape(N_LEV, N_ROW, 256)
    level_recv[my_lev] = level_send[my_lev]

    @pl.loop(1, N_LEV)
    def _(k):
        other = lax.rem(my_lev + k, N_LEV)
        pltpu.make_async_remote_copy(
            level_send.at[other], level_recv.at[my_lev], cs_sem.at[0], cr_sem.at[0],
            device_id=(other, my_row), device_id_type=MESH,
        ).start()

    def all_but_one(send, recv, n, slot):
        return pltpu.make_async_remote_copy(
            send.at[pl.ds(0, n - 1)], recv.at[pl.ds(0, n - 1)], cs_sem.at[slot], cr_sem.at[slot],
            device_id=(my_lev, up_row), device_id_type=MESH,
        )

    levels = all_but_one(level_send, level_recv, N_LEV, 0)
    levels.wait_recv()
    total = jnp.sum(level_recv[...], axis=0)
    row_send[:, 0, :] = total[:, :128]
    row_send[:, 1, :] = total[:, 128:]
    row_recv[my_row] = row_send[my_row]

    @pl.loop(1, N_ROW)
    def _(k):
        other = lax.rem(my_row + k, N_ROW)
        pltpu.make_async_remote_copy(
            row_send.at[other], row_recv.at[my_row], cs_sem.at[1], cr_sem.at[1],
            device_id=(my_lev, other), device_id_type=MESH,
        ).start()

    last = all_but_one(row_send, row_recv, N_ROW, 1)
    last.wait_recv()
    inv[...] = jnp.sum(row_recv[...], axis=0)
    inv_copy = pltpu.make_async_copy(inv, inv_out, out_sem.at[3])
    inv_copy.start()
    levels.wait_send()
    last.wait_send()
    for w in range(4):
        wave(w, 31 if w == 0 else 32).wait_send()
    final_copy.wait()
    adj_copy.wait()
    cross_copy.wait()
    inv_copy.wait()


def write_out(*refs):
    stages = [], []
    for a, b, held in zip(refs[:4], refs[4:8], refs[8:12]):
        rows = a.shape[0]
        step = min(rows, 512)
        for at in range(0, rows, step):
            for n, (src, dst) in enumerate(((a, held), (held, b))):
                here = pl.ds(at, step)
                stages[n].append(pltpu.make_async_copy(src.at[here], dst.at[here], refs[12].at[n, len(stages[n])]))
    for c in stages[0]:
        c.start()
    for c, d in zip(*stages):
        c.wait()
        d.start()
    for d in stages[1]:
        d.wait()


def rows_of(slab):
    return slab.reshape(16, 4, 32, 128).transpose(0, 2, 1, 3).reshape(ROWS, 128)


def local(
    tracer, courant_x, courant_y, wind_x, wind_y, inverse_diffusion,
    receptor_cell, receptor_limit, stack_cell, stack_dest, stack_slot, stack_weight,
):
    hbm = pl.BlockSpec(memory_space=pl.ANY)
    slab = pltpu.VMEM((ROWS, 128), F32)
    dma = pltpu.SemaphoreType.DMA
    blocks = pltpu.VMEM((N, 16, 128), F32)
    edge = pltpu.VMEM((2, 4, 128, 128), F32)
    results = pl.pallas_call(
        kernel,
        out_shape=(
            jax.ShapeDtypeStruct((ROWS, 128), F32),
            jax.ShapeDtypeStruct((16, 128), F32),
            jax.ShapeDtypeStruct((ROWS, 128), F32),
            jax.ShapeDtypeStruct((2, 128), F32),
        ),
        in_specs=[hbm] * 12,
        out_specs=(hbm,) * 4,
        scratch_shapes=[
            slab, slab, slab, pltpu.VMEM((ROWS, 128), I32), pltpu.VMEM((ROWS, 128), I32), pltpu.VMEM((32, 128, 128), F32),
            pltpu.VMEM((16, 128), I32), pltpu.VMEM((16, 128), F32), pltpu.VMEM((4, 128), I32), pltpu.VMEM((4, 128), I32),
            pltpu.VMEM((4, 128), I32), pltpu.VMEM((4, 128), F32), pltpu.VMEM((16, 128), F32), pltpu.VMEM((2, 128), F32),
            slab, slab, slab, pltpu.VMEM((ROWS, 256), BF16),
            pltpu.VMEM((ROWS, 256), BF16), blocks, blocks, blocks,
            pltpu.VMEM((N_LEV, N_ROW, 256), F32), pltpu.VMEM((N_LEV, N_ROW, 256), F32),
            pltpu.VMEM((N_ROW, 2, 128), F32), pltpu.VMEM((N_ROW, 2, 128), F32),
            edge, edge, edge, edge, pltpu.VMEM((16, 128), F32),
            dma((12,)), dma, dma((4,)), dma((4, 4)), dma((4, 4)), dma, dma, dma((4,)), dma((4,)), dma((2,)), dma((2,)), pltpu.SemaphoreType.REGULAR,
        ],
        compiler_params=pltpu.CompilerParams(
            collective_id=0, has_side_effects=True, vmem_limit_bytes=56 * 1024 * 1024
        ),
        name="transport",
    )(
        rows_of(tracer), rows_of(courant_x), rows_of(courant_y), rows_of(wind_x), rows_of(wind_y), inverse_diffusion,
        receptor_cell.reshape(16, 128), receptor_limit.reshape(16, 128), stack_cell.reshape(4, 128),
        stack_dest.reshape(4, 128), stack_slot.reshape(4, 128), stack_weight.reshape(4, 128),
    )
    final_field, crossing, adjoint, inventory = pl.pallas_call(
        write_out,
        out_shape=tuple(jax.ShapeDtypeStruct(r.shape, r.dtype) for r in results),
        in_specs=[hbm] * 4,
        out_specs=(hbm,) * 4,
        scratch_shapes=[pltpu.VMEM(r.shape, r.dtype) for r in results] + [dma((2, 10))],
        name="write_out",
    )(*results)
    adjoint = adjoint.reshape(16, 32, 4, 128).transpose(0, 2, 1, 3).reshape(16, 4, 4096)
    return final_field.reshape(32, 64, 128), crossing.reshape(-1), adjoint, inventory.reshape(-1)


def solution(mesh):
    slab = P("lev", "row", None)
    flat = P(("lev", "row"))
    return jax.shard_map(
        local,
        mesh=mesh,
        in_specs=(slab,) * 5 + (P(("lev", "row"), None, None), flat, flat, flat, P(("lev", "row"), None), flat, flat),
        out_specs=(P(("lev", "row"), None, None), flat, slab, flat),
        check_vma=False,
    )
```

```python
import functools

import jax
import jax.numpy as jnp
from jax import lax
from jax.experimental import pallas as pl
from jax.experimental.pallas import tpu as pltpu
from jax.sharding import PartitionSpec as P

F32 = jnp.float32
BF16 = jnp.bfloat16
I32 = jnp.int32
MESH = pl.DeviceIdType.MESH
N_LEV = 8
N_ROW = 16
N = N_LEV * N_ROW
ROWS = 2048
TILE = 1024


def place(d):
    return (d // N_ROW, lax.rem(d, N_ROW))


def iota(shape, dim):
    return lax.broadcasted_iota(I32, shape, dim)


def swap4(v, unit):
    lane = iota(v[0].shape, 1)
    for bit in (1, 2):
        step = unit * bit
        high = (lane & step) != 0
        out = list(v)
        for a in range(4):
            if a & bit:
                continue
            b = a | bit
            out[a] = jnp.where(high, pltpu.roll(v[b], step, 1), v[a])
            out[b] = jnp.where(high, v[b], pltpu.roll(v[a], 128 - step, 1))
        v = out
    return v


def as_column(row):
    return jnp.broadcast_to(row, (128, 128)).T


def as_row(column):
    eye = iota((128, 128), 0) == iota((128, 128), 1)
    return jnp.sum(jnp.where(eye, jnp.broadcast_to(column, (128, 128)), 0.0), axis=0, keepdims=True)


def halves(v):
    high = v.astype(BF16)
    return high, (v - high.astype(F32)).astype(BF16)


def dot(a, b, dims):
    return lax.dot_general(a, b, (dims, ((), ())), preferred_element_type=F32)


def dot_split(a, b, dims):
    n = a.shape[0]
    side = 0 if dims[1] == (1,) else 1
    g = dot(jnp.concatenate(halves(a), axis=0), jnp.concatenate(halves(b), axis=side), dims)
    return (g[:n, :128] + g[n:, :128]) + (g[:n, 128:] + g[n:, 128:])


def one_hot(mask):
    return jnp.where(mask, 1.0, 0.0).astype(BF16)


def kernel(
    t_in, cx_in, cy_in, sx_in, sy_in, mat_in, rcell_in, rlim_in, scell_in, sdest_in, sslot_in, swt_in,
    final_out, cross_out, adj_out, inv_out,
    t, cx, cy, sx, sy, mat, rcell, rlim, scell, sdest, sslot, swt, cross, inv, work, cols, field, parts, values, send_a, recv_a, recv_b, level_send, level_recv, row_send, row_recv,
    halo_send, halo_recv, hback_send, hback_recv, picked,
    load_sem, own_sem, out_sem, hs_sem, hr_sem, as_sem, ar_sem, bs_sem, br_sem, cs_sem, cr_sem, ready,
):
    my_lev = lax.axis_index("lev")
    my_row = lax.axis_index("row")
    me = my_lev * N_ROW + my_row
    up_row = lax.rem(my_row + 1, N_ROW)
    down_row = lax.rem(my_row + N_ROW - 1, N_ROW)

    loads = []
    inputs = (
        (t_in, t), (cx_in, cx), (cy_in, cy), (sx_in, sx), (sy_in, sy), (mat_in, mat), (rcell_in, rcell),
        (rlim_in, rlim), (scell_in, scell), (sdest_in, sdest), (sslot_in, sslot), (swt_in, swt),
    )
    for n, (src, dst) in enumerate(inputs):
        c = pltpu.make_async_copy(src, dst, load_sem.at[n])
        c.start()
        loads.append(c)

    barrier = pltpu.get_barrier_semaphore()

    @pl.loop(1, N_ROW)
    def _(k):
        other = (my_lev, lax.rem(my_row + k, N_ROW))
        pl.semaphore_signal(barrier, inc=1, device_id=other, device_id_type=MESH)

    @pl.loop(1, N_LEV)
    def _(k):
        other = (lax.rem(my_lev + k, N_LEV), my_row)
        pl.semaphore_signal(barrier, inc=1, device_id=other, device_id_type=MESH)

    loads[0].wait()
    tile_row = iota((128, 128), 0)
    tile_lane = iota((128, 128), 1)
    tile_low = (tile_row & 4) == 0

    def exchange_halves(a, b):
        return jnp.where(tile_low, a, pltpu.roll(b, 4, 0)), jnp.where(tile_low, pltpu.roll(a, 124, 0), b)

    for slot, start in ((0, 3), (1, 0)):
        edge = t[pl.ds(start, 512, stride=4), :].reshape(16, 4, 8, 128)
        for n in range(2):
            a, b = exchange_halves(edge[:, n].reshape(128, 128), edge[:, n + 2].reshape(128, 128))
            halo_send[slot, 2 * n] = a
            halo_send[slot, 2 * n + 1] = b

    def piece(w):
        return 2 * lax.rem(my_lev // 2 + w // 2, 2) + lax.rem(my_lev + w, 2)

    def pair_of(p, n):
        return 2 * p + lax.rem(n, 2) + 8 * (n // 2)

    pl.semaphore_wait(barrier, N_ROW + N_LEV - 2)

    @pl.loop(1, N_ROW)
    def _(k):
        other = (my_lev, lax.rem(my_row + k, N_ROW))
        pl.semaphore_signal(ready, inc=1, device_id=other, device_id_type=MESH)


    def exchange(send, recv, base, slot, p):
        return pltpu.make_async_remote_copy(
            send.at[slot, p], recv.at[slot, p], hs_sem.at[base + slot, p], hr_sem.at[base + slot, p],
            device_id=(my_lev, (up_row, down_row)[slot]), device_id_type=MESH,
        )

    @pl.loop(0, 4)
    def _(w):
        for slot in range(2):
            exchange(halo_send, halo_recv, 0, slot, piece(w)).start()

    for c in loads[1:5]:
        c.wait()

    strip_row = tile_row & 3

    def from_left(v):
        rolled = pltpu.roll(v, 1, 1)
        carried = jnp.where(tile_row < 4, 0.0, pltpu.roll(rolled, 4, 0))
        return jnp.where(tile_lane == 0, carried, rolled)

    def from_right(v):
        rolled = pltpu.roll(v, 127, 1)
        carried = jnp.where(tile_row >= 124, 0.0, pltpu.roll(rolled, 124, 0))
        return jnp.where(tile_lane == 127, carried, rolled)

    def from_before(v):
        return jnp.where(strip_row == 0, 0.0, pltpu.roll(v, 1, 0))

    def from_after(v):
        return jnp.where(strip_row == 3, 0.0, pltpu.roll(v, 127, 0))

    @pl.loop(0, 16)
    def _(lev):
        at = pl.ds(pl.multiple_of(lev * 128, 128), 128)
        v, a, b = t[at], cx[at], cy[at]
        work[at] = (
            (1.0 - a - b) * v
            + a * jnp.where(sx[at] != 0, from_before(v), from_after(v))
            + b * jnp.where(sy[at] != 0, from_left(v), from_right(v))
        )

    has_down = jnp.where(my_row > 0, 1.0, 0.0)
    has_up = jnp.where(my_row < N_ROW - 1, 1.0, 0.0)

    def edge_rows(lev, half, p, r):
        return pl.ds(lev * 128 + half * 64 + p * 16 + r, 4, stride=4), pl.ds(lev * 8 + half * 4, 4)

    pl.semaphore_wait(ready, N_ROW - 1)

    low = iota((8, 128), 0) < 4
    here = my_row * N_LEV + my_lev

    @pl.loop(0, 4)
    def _(w):
        p = piece(w)
        for slot in range(2):
            exchange(halo_send, halo_recv, 0, slot, p).wait()
        for lev in range(16):
            for half in range(2):
                e, at = edge_rows(lev, half, p, 0)
                v = cx[e, :] * halo_recv[0, p, at]
                work[e, :] = work[e, :] + has_down * jnp.where(sx[e, :] != 0, v, 0.0)
                e, at = edge_rows(lev, half, p, 3)
                v = cx[e, :] * halo_recv[1, p, at]
                work[e, :] = work[e, :] + has_up * jnp.where(sx[e, :] != 0, 0.0, v)

        @pl.loop(0, 4)
        def _(k):
            pair = pair_of(p, lax.rem(k + 2 * (my_lev // 4) + my_row // 8, 4))
            at = pl.multiple_of(pair * 8, 8)
            groups = []
            for group in range(4):
                v = [work[pl.ds(pl.multiple_of((group * 4 + g) * 128 + at, 8), 8), :] for g in range(4)]
                groups.append(swap4(v, 32))
            for half in range(2):
                for q in range(4):
                    a, b = groups[half * 2][q], groups[half * 2 + 1][q]
                    send_a[at + q, half * 8:half * 8 + 8] = jnp.where(low, a, pltpu.roll(b, 4, 0))
                    send_a[at + 4 + q, half * 8:half * 8 + 8] = jnp.where(low, pltpu.roll(a, 4, 0), b)

            @pl.loop(0, 8)
            def _(e):
                @pl.when(w + k + e > 0)
                def _():
                    other = at + lax.rem(e + me, 8)
                    pltpu.make_async_remote_copy(
                        send_a.at[other], recv_a.at[here], as_sem, ar_sem, device_id=place(other), device_id_type=MESH
                    ).start()

                @pl.when(w + k + e == 0)
                def _():
                    pltpu.make_async_copy(send_a.at[me], recv_a.at[here], own_sem).start()

    def all_of(send, recv, ss, rs):
        return pltpu.make_async_remote_copy(
            send.at[pl.ds(0, N - 1)], recv.at[pl.ds(0, N - 1)], ss, rs,
            device_id=(my_lev, up_row), device_id_type=MESH,
        )

    for c in loads[5:]:
        c.wait()
    pltpu.make_async_copy(send_a.at[me], recv_a.at[here], own_sem).wait()
    flow = all_of(send_a, recv_a, as_sem, ar_sem)
    flow.wait_recv()

    @pl.loop(0, 16, unroll=2)
    def _(j):
        v = recv_a[pl.ds(j * 8, 8)].reshape(128, 128).T
        for r, u in enumerate(swap4([v[g * 32:g * 32 + 32] for g in range(4)], 1)):
            cols[pl.ds(pl.multiple_of(j * 128 + r * 32, 32), 32), :] = u

    @pl.loop(0, 32, unroll=4)
    def _(y):
        v = dot_split(cols[pl.ds(y, 64, stride=32), :], mat[y], ((1,), (1,)))
        at = pl.ds(pl.multiple_of(y * 64, 64), 64)
        field[at] = v
        h, l = halves(v)
        parts[at, 0:128] = h
        parts[at, 128:256] = l

    final_copy = pltpu.make_async_copy(field, final_out, out_sem.at[0])
    final_copy.start()

    def column(ref, base, tile):
        return jnp.concatenate([as_column(ref(base + s)) for s in range(tile // 128)], axis=0)

    def pick(base, tile, row_of, lane_of, out):
        lanes = iota((tile, 128), 1)
        rows = column(row_of, base, tile)
        g = jnp.zeros((tile, 256), F32)
        for k in range(8):
            h = jnp.concatenate([one_hot(rows == lanes + (k * 256 + half)) for half in (0, 128)], axis=1)
            g = g + dot(h, parts[k * 256:k * 256 + 256], ((1,), (0,)))
        mask = column(lane_of, base, tile) == lanes
        g = jnp.sum(jnp.where(mask, g[:, :128] + g[:, 128:], 0.0), axis=1, keepdims=True)
        for s in range(tile // 128):
            out[pl.ds(base + s, 1), :] = as_row(g[s * 128:s * 128 + 128])
        return mask

    @pl.loop(0, 2)
    def _(u):
        mask = pick(u * 8, TILE, lambda s: rcell[pl.ds(s, 1), :] >> 7, lambda s: rcell[pl.ds(s, 1), :] & 127, picked)
        work[pl.ds(pl.multiple_of(u * TILE, TILE), TILE), :] = jnp.where(mask, 1.0, 0.0)

    crossing = jax.nn.sigmoid(2.0 * (picked[...] - rlim[...]))
    cross[...] = crossing
    cross_copy = pltpu.make_async_copy(cross, cross_out, out_sem.at[2])
    cross_copy.start()
    picked[...] = 2.0 * crossing * (1.0 - crossing)

    @pl.loop(0, 16, unroll=2)
    def _(u):
        at = pl.ds(pl.multiple_of(u * 128, 128), 128)
        h, l = halves(work[at] * as_column(picked[pl.ds(u, 1), :]))
        values[at, 0:128] = h
        values[at, 128:256] = l

    @pl.loop(0, 2)
    def _(u):
        rows = iota((TILE, 128), 0) + u * TILE
        g = jnp.zeros((TILE, 256), F32)
        for k in range(8):
            h = jnp.concatenate([one_hot((rcell[2 * k + n:2 * k + n + 1, :] >> 7) == rows) for n in (0, 1)], axis=1)
            g = g + dot(h, values[k * 256:k * 256 + 256], ((1,), (0,)))
        work[pl.ds(pl.multiple_of(u * TILE, TILE), TILE), :] = g[:, :128] + g[:, 128:]

    @pl.loop(0, 32, unroll=4)
    def _(y):
        at = pl.ds(pl.multiple_of(y * 64, 64), 64)
        cols[pl.ds(y, 64, stride=32), :] = dot_split(work[at], mat[y], ((1,), (0,)))

    flow.wait_send()

    def send_back(w, j, n):
        i = piece(w) + 4 * lax.rem(my_lev // 4 + n, 2)
        block = j * N_LEV + i
        at_home = (i == my_lev) & (j == my_row)

        @pl.when(jnp.logical_not(at_home))
        def _():
            pltpu.make_async_remote_copy(
                send_a.at[block], recv_b.at[me], bs_sem.at[w], br_sem.at[w], device_id=(i, j), device_id_type=MESH
            ).start()

        @pl.when(at_home)
        def _():
            pltpu.make_async_copy(send_a.at[here], recv_b.at[me], own_sem).start()

    @pl.loop(0, 16)
    def _(k):
        j = lax.rem(5 * k + my_row, N_ROW)
        v = [cols[pl.ds(pl.multiple_of(j * 128 + r * 32, 32), 32), :] for r in range(4)]
        v = jnp.concatenate(swap4(v, 1), axis=0).T
        send_a[pl.ds(j * 8, 8)] = v.reshape(8, 16, 128)

        for n in range(2):
            send_back(0, j, n)

    @pl.loop(1, 4)
    def _(w):
        @pl.loop(0, 16)
        def _(k):
            for n in range(2):
                send_back(w, lax.rem(5 * k + my_row, N_ROW), n)

    def wave(w, n):
        return pltpu.make_async_remote_copy(
            send_a.at[pl.ds(0, n)], recv_b.at[pl.ds(0, n)], bs_sem.at[w], br_sem.at[w],
            device_id=(my_lev, up_row), device_id_type=MESH,
        )

    pltpu.make_async_copy(send_a.at[here], recv_b.at[me], own_sem).wait()
    for w in range(4):
        wave(w, 31 if w == 0 else 32).wait_recv()
        p = piece(w)

        @pl.loop(0, 4)
        def _(k):
            at = pl.multiple_of(pair_of(p, k) * 8, 8)
            for half in range(2):
                va, vb = [], []
                for q in range(4):
                    u = recv_b[at + q, half * 8:half * 8 + 8]
                    s = recv_b[at + 4 + q, half * 8:half * 8 + 8]
                    va.append(jnp.where(low, u, pltpu.roll(s, 4, 0)))
                    vb.append(jnp.where(low, pltpu.roll(u, 4, 0), s))
                for group, v in ((half * 2, va), (half * 2 + 1, vb)):
                    for g, u in enumerate(swap4(v, 32)):
                        t[pl.ds(pl.multiple_of((group * 4 + g) * 128 + at, 8), 8), :] = u

        for lev in range(16):
            for half in range(2):
                e, at = edge_rows(lev, half, p, 3)
                hback_send[0, p, at] = jnp.where(sx[e, :] != 0, 0.0, cx[e, :] * t[e, :])
                e, at = edge_rows(lev, half, p, 0)
                hback_send[1, p, at] = jnp.where(sx[e, :] != 0, cx[e, :] * t[e, :], 0.0)
        for slot in range(2):
            exchange(hback_send, hback_recv, 2, slot, p).start()

    @pl.loop(0, 16)
    def _(lev):
        at = pl.ds(pl.multiple_of(lev * 128, 128), 128)
        v, a, b = t[at], cx[at], cy[at]
        flux_x, flux_y = a * v, b * v
        lower_x, lower_y = sx[at] != 0, sy[at] != 0
        work[at] = (
            (1.0 - a - b) * v
            + from_after(jnp.where(lower_x, flux_x, 0.0))
            + from_before(jnp.where(lower_x, 0.0, flux_x))
            + from_right(jnp.where(lower_y, flux_y, 0.0))
            + from_left(jnp.where(lower_y, 0.0, flux_y))
        )

    for p in range(4):
        for slot in range(2):
            exchange(hback_send, hback_recv, 2, slot, p).wait()

    def edge_of(slot):
        v = exchange_halves(hback_recv[slot, 0], hback_recv[slot, 1])
        u = exchange_halves(hback_recv[slot, 2], hback_recv[slot, 3])
        v = (v[0], u[0], v[1], u[1])
        return jnp.concatenate([x[lev * 8:lev * 8 + 8] for lev in range(16) for x in v], axis=0)

    first = pl.ds(0, 512, stride=4)
    final = pl.ds(3, 512, stride=4)
    work[first, :] = work[first, :] + has_down * edge_of(0)
    work[final, :] = work[final, :] + has_up * edge_of(1)
    adj_copy = pltpu.make_async_copy(work, adj_out, out_sem.at[1])
    adj_copy.start()

    @pl.loop(0, 16)
    def _(lev):
        at = pl.ds(pl.multiple_of(lev * 128, 128), 128)
        h, l = halves(work[at])
        parts[at, 0:128] = h
        parts[at, 128:256] = l

    def stack_row(s):
        c = scell[pl.ds(s, 1), :]
        return (c >> 14) * 128 + ((c >> 7) & 31) * 4 + ((c >> 12) & 3)

    pick(0, 512, stack_row, lambda s: scell[pl.ds(s, 1), :] & 127, picked)
    stack_values = picked[0:4, :] * swt[...]
    partial = jnp.zeros((128, 256), F32)
    wide = iota((128, 256), 1)
    for s in range(4):
        owner = one_hot(sdest[s:s + 1, :] == tile_row)
        slot = as_column(sslot[s:s + 1, :])
        amount = as_column(stack_values[s:s + 1, :])
        slot = jnp.concatenate([slot, slot], axis=1)
        amount = jnp.concatenate([amount, amount], axis=1)
        h, l = halves(jnp.where(slot == wide, amount, 0.0))
        partial = partial + (dot(owner, h, ((1,), (0,))) + dot(owner, l, ((1,), (0,))))
    level_send[...] = partial.reshape(N_LEV, N_ROW, 256)
    level_recv[my_lev] = level_send[my_lev]

    @pl.loop(1, N_LEV)
    def _(k):
        other = lax.rem(my_lev + k, N_LEV)
        pltpu.make_async_remote_copy(
            level_send.at[other], level_recv.at[my_lev], cs_sem.at[0], cr_sem.at[0],
            device_id=(other, my_row), device_id_type=MESH,
        ).start()

    def all_but_one(send, recv, n, slot):
        return pltpu.make_async_remote_copy(
            send.at[pl.ds(0, n - 1)], recv.at[pl.ds(0, n - 1)], cs_sem.at[slot], cr_sem.at[slot],
            device_id=(my_lev, up_row), device_id_type=MESH,
        )

    levels = all_but_one(level_send, level_recv, N_LEV, 0)
    levels.wait_recv()
    total = jnp.sum(level_recv[...], axis=0)
    row_send[:, 0, :] = total[:, :128]
    row_send[:, 1, :] = total[:, 128:]
    row_recv[my_row] = row_send[my_row]

    @pl.loop(1, N_ROW)
    def _(k):
        other = lax.rem(my_row + k, N_ROW)
        pltpu.make_async_remote_copy(
            row_send.at[other], row_recv.at[my_row], cs_sem.at[1], cr_sem.at[1],
            device_id=(my_lev, other), device_id_type=MESH,
        ).start()

    last = all_but_one(row_send, row_recv, N_ROW, 1)
    last.wait_recv()
    inv[...] = jnp.sum(row_recv[...], axis=0)
    inv_copy = pltpu.make_async_copy(inv, inv_out, out_sem.at[3])
    inv_copy.start()
    levels.wait_send()
    last.wait_send()
    for w in range(4):
        wave(w, 31 if w == 0 else 32).wait_send()
    final_copy.wait()
    adj_copy.wait()
    cross_copy.wait()
    inv_copy.wait()


def write_out(*refs):
    stages = [], []
    for a, b, held in zip(refs[:4], refs[4:8], refs[8:12]):
        rows = a.shape[0]
        step = min(rows, 512)
        for at in range(0, rows, step):
            for n, (src, dst) in enumerate(((a, held), (held, b))):
                here = pl.ds(at, step)
                stages[n].append(pltpu.make_async_copy(src.at[here], dst.at[here], refs[12].at[n, len(stages[n])]))
    for c in stages[0]:
        c.start()
    for c, d in zip(*stages):
        c.wait()
        d.start()
    for d in stages[1]:
        d.wait()


def rows_of(slab):
    return slab.reshape(16, 4, 32, 128).transpose(0, 2, 1, 3).reshape(ROWS, 128)


def local(
    tracer, courant_x, courant_y, wind_x, wind_y, inverse_diffusion,
    receptor_cell, receptor_limit, stack_cell, stack_dest, stack_slot, stack_weight,
):
    hbm = pl.BlockSpec(memory_space=pl.ANY)
    slab = pltpu.VMEM((ROWS, 128), F32)
    dma = pltpu.SemaphoreType.DMA
    blocks = pltpu.VMEM((N, 16, 128), F32)
    edge = pltpu.VMEM((2, 4, 128, 128), F32)
    results = pl.pallas_call(
        kernel,
        out_shape=(
            jax.ShapeDtypeStruct((ROWS, 128), F32),
            jax.ShapeDtypeStruct((16, 128), F32),
            jax.ShapeDtypeStruct((ROWS, 128), F32),
            jax.ShapeDtypeStruct((2, 128), F32),
        ),
        in_specs=[hbm] * 12,
        out_specs=(hbm,) * 4,
        scratch_shapes=[
            slab, slab, slab, pltpu.VMEM((ROWS, 128), I32), pltpu.VMEM((ROWS, 128), I32), pltpu.VMEM((32, 128, 128), F32),
            pltpu.VMEM((16, 128), I32), pltpu.VMEM((16, 128), F32), pltpu.VMEM((4, 128), I32), pltpu.VMEM((4, 128), I32),
            pltpu.VMEM((4, 128), I32), pltpu.VMEM((4, 128), F32), pltpu.VMEM((16, 128), F32), pltpu.VMEM((2, 128), F32),
            slab, slab, slab, pltpu.VMEM((ROWS, 256), BF16),
            pltpu.VMEM((ROWS, 256), BF16), blocks, blocks, blocks,
            pltpu.VMEM((N_LEV, N_ROW, 256), F32), pltpu.VMEM((N_LEV, N_ROW, 256), F32),
            pltpu.VMEM((N_ROW, 2, 128), F32), pltpu.VMEM((N_ROW, 2, 128), F32),
            edge, edge, edge, edge, pltpu.VMEM((16, 128), F32),
            dma((12,)), dma, dma((4,)), dma((4, 4)), dma((4, 4)), dma, dma, dma((4,)), dma((4,)), dma((2,)), dma((2,)), pltpu.SemaphoreType.REGULAR,
        ],
        compiler_params=pltpu.CompilerParams(
            collective_id=0, has_side_effects=True, vmem_limit_bytes=56 * 1024 * 1024
        ),
        name="transport",
    )(
        rows_of(tracer), rows_of(courant_x), rows_of(courant_y), rows_of(wind_x), rows_of(wind_y), inverse_diffusion,
        receptor_cell.reshape(16, 128), receptor_limit.reshape(16, 128), stack_cell.reshape(4, 128),
        stack_dest.reshape(4, 128), stack_slot.reshape(4, 128), stack_weight.reshape(4, 128),
    )
    final_field, crossing, adjoint, inventory = pl.pallas_call(
        write_out,
        out_shape=tuple(jax.ShapeDtypeStruct(r.shape, r.dtype) for r in results),
        in_specs=[hbm] * 4,
        out_specs=(hbm,) * 4,
        scratch_shapes=[pltpu.VMEM(r.shape, r.dtype) for r in results] + [dma((2, 10))],
        name="write_out",
    )(*results)
    adjoint = adjoint.reshape(16, 32, 4, 128).transpose(0, 2, 1, 3).reshape(16, 4, 4096)
    return final_field.reshape(32, 64, 128), crossing.reshape(-1), adjoint, inventory.reshape(-1)


def solution(mesh):
    slab = P("lev", "row", None)
    flat = P(("lev", "row"))
    return jax.shard_map(
        local,
        mesh=mesh,
        in_specs=(slab,) * 5 + (P(("lev", "row"), None, None), flat, flat, flat, P(("lev", "row"), None), flat, flat),
        out_specs=(P(("lev", "row"), None, None), flat, slab, flat),
        check_vma=False,
    )
```

```python
import functools

import jax
import jax.numpy as jnp
from jax import lax
from jax.experimental import pallas as pl
from jax.experimental.pallas import tpu as pltpu
from jax.sharding import PartitionSpec as P

F32 = jnp.float32
BF16 = jnp.bfloat16
I32 = jnp.int32
MESH = pl.DeviceIdType.MESH
N_LEV = 8
N_ROW = 16
N = N_LEV * N_ROW
ROWS = 2048
PITCH = 40
TILE = 1024


def place(d):
    return (d // N_ROW, lax.rem(d, N_ROW))


def iota(shape, dim):
    return lax.broadcasted_iota(I32, shape, dim)


def swap4(v, unit):
    lane = iota(v[0].shape, 1)
    for bit in (1, 2):
        step = unit * bit
        high = (lane & step) != 0
        out = list(v)
        for a in range(4):
            if a & bit:
                continue
            b = a | bit
            out[a] = jnp.where(high, pltpu.roll(v[b], step, 1), v[a])
            out[b] = jnp.where(high, v[b], pltpu.roll(v[a], 128 - step, 1))
        v = out
    return v


def as_column(row):
    return jnp.broadcast_to(row, (128, 128)).T


def as_row(column):
    eye = iota((128, 128), 0) == iota((128, 128), 1)
    return jnp.sum(jnp.where(eye, jnp.broadcast_to(column, (128, 128)), 0.0), axis=0, keepdims=True)


def halves(v):
    high = v.astype(BF16)
    return high, (v - high.astype(F32)).astype(BF16)


def dot(a, b, dims):
    return lax.dot_general(a, b, (dims, ((), ())), preferred_element_type=F32)


def dot_split(a, b):
    n = a.shape[0]
    g = dot(jnp.concatenate(halves(a), axis=0), b, ((1,), (0,)))
    return (g[:n, :128] + g[n:, :128]) + (g[:n, 128:] + g[n:, 128:])


def one_hot(mask):
    return jnp.where(mask, 1.0, 0.0).astype(BF16)


def kernel(
    t_in, cx_in, cy_in, sx_in, sy_in, mat_in, rcell_in, rlim_in, scell_in, sdest_in, sslot_in, swt_in,
    final_out, cross_out, adj_out, inv_out,
    t, cx, cy, sx, sy, mat, rcell, rlim, scell, sdest, sslot, swt, cross, inv,
    mat_fwd, mat_back, hot, hot_turned, work, cols, field, parts, values, send_a, recv_a, recv_b, owner_send, owner_recv, core_send, core_recv,
    halo_send, halo_recv, hback_send, hback_recv, picked,
    load_sem, own_sem, out_sem, hs_sem, hr_sem, as_sem, ar_sem, bs_sem, br_sem, cs_sem, cr_sem, ps_sem, pr_sem, ready,
):
    my_lev = lax.axis_index("lev")
    my_row = lax.axis_index("row")
    my_y = my_lev // 2
    me = my_lev * N_ROW + my_row
    up_row = lax.rem(my_row + 1, N_ROW)
    down_row = lax.rem(my_row + N_ROW - 1, N_ROW)

    loads = []
    inputs = (
        (t_in, t), (cx_in, cx), (cy_in, cy), (sx_in, sx), (sy_in, sy), (mat_in, mat), (rcell_in, rcell),
        (rlim_in, rlim), (scell_in, scell), (sdest_in, sdest), (sslot_in, sslot), (swt_in, swt),
    )
    for n, (src, dst) in enumerate(inputs):
        c = pltpu.make_async_copy(src, dst, load_sem.at[n])
        c.start()
        loads.append(c)

    barrier = pltpu.get_barrier_semaphore()

    @pl.loop(1, N_ROW)
    def _(k):
        other = (my_lev, lax.rem(my_row + k, N_ROW))
        pl.semaphore_signal(barrier, inc=1, device_id=other, device_id_type=MESH)

    @pl.loop(1, N_LEV)
    def _(k):
        other = (lax.rem(my_lev + k, N_LEV), my_row)
        pl.semaphore_signal(barrier, inc=1, device_id=other, device_id_type=MESH)

    loads[0].wait()
    tile_row = iota((128, 128), 0)
    tile_lane = iota((128, 128), 1)
    tile_low = (tile_row & 4) == 0

    def exchange_halves(a, b):
        return jnp.where(tile_low, a, pltpu.roll(b, 4, 0)), jnp.where(tile_low, pltpu.roll(a, 124, 0), b)

    for slot, start in ((0, 3), (1, 0)):
        edge = t[pl.ds(start, 512, stride=4), :].reshape(16, 4, 8, 128)
        for n in range(2):
            a, b = exchange_halves(edge[:, n].reshape(128, 128), edge[:, n + 2].reshape(128, 128))
            halo_send[slot, 2 * n] = a
            halo_send[slot, 2 * n + 1] = b

    def piece(w):
        return 2 * lax.rem(my_lev // 2 + w // 2, 2) + lax.rem(my_lev + w, 2)

    def pair_of(p, n):
        return 2 * p + lax.rem(n, 2) + 8 * (n // 2)

    pl.semaphore_wait(barrier, N_ROW + N_LEV - 2)

    @pl.loop(1, N_ROW)
    def _(k):
        other = (my_lev, lax.rem(my_row + k, N_ROW))
        pl.semaphore_signal(ready, inc=1, device_id=other, device_id_type=MESH)


    def exchange(send, recv, base, slot, p):
        return pltpu.make_async_remote_copy(
            send.at[slot, p], recv.at[slot, p], hs_sem.at[base + slot, p], hr_sem.at[base + slot, p],
            device_id=(my_lev, (up_row, down_row)[slot]), device_id_type=MESH,
        )

    @pl.loop(0, 4)
    def _(w):
        for slot in range(2):
            exchange(halo_send, halo_recv, 0, slot, piece(w)).start()

    for c in loads[1:5]:
        c.wait()

    strip_row = tile_row & 3

    def from_left(v):
        rolled = pltpu.roll(v, 1, 1)
        carried = jnp.where(tile_row < 4, 0.0, pltpu.roll(rolled, 4, 0))
        return jnp.where(tile_lane == 0, carried, rolled)

    def from_right(v):
        rolled = pltpu.roll(v, 127, 1)
        carried = jnp.where(tile_row >= 124, 0.0, pltpu.roll(rolled, 124, 0))
        return jnp.where(tile_lane == 127, carried, rolled)

    def from_before(v):
        return jnp.where(strip_row == 0, 0.0, pltpu.roll(v, 1, 0))

    def from_after(v):
        return jnp.where(strip_row == 3, 0.0, pltpu.roll(v, 127, 0))

    @pl.loop(0, 16)
    def _(lev):
        at = pl.ds(pl.multiple_of(lev * 128, 128), 128)
        v, a, b = t[at], cx[at], cy[at]
        work[at] = (
            (1.0 - a - b) * v
            + a * jnp.where(sx[at] != 0, from_before(v), from_after(v))
            + b * jnp.where(sy[at] != 0, from_left(v), from_right(v))
        )

    has_down = jnp.where(my_row > 0, 1.0, 0.0)
    has_up = jnp.where(my_row < N_ROW - 1, 1.0, 0.0)

    def edge_rows(lev, half, p, r):
        return pl.ds(lev * 128 + half * 64 + p * 16 + r, 4, stride=4), pl.ds(lev * 8 + half * 4, 4)

    pl.semaphore_wait(ready, N_ROW - 1)

    low = iota((8, 128), 0) < 4
    here = my_row * N_LEV + my_lev

    @pl.loop(0, 4)
    def _(w):
        p = piece(w)
        for slot in range(2):
            exchange(halo_send, halo_recv, 0, slot, p).wait()
        for lev in range(16):
            for half in range(2):
                e, at = edge_rows(lev, half, p, 0)
                v = cx[e, :] * halo_recv[0, p, at]
                work[e, :] = work[e, :] + has_down * jnp.where(sx[e, :] != 0, v, 0.0)
                e, at = edge_rows(lev, half, p, 3)
                v = cx[e, :] * halo_recv[1, p, at]
                work[e, :] = work[e, :] + has_up * jnp.where(sx[e, :] != 0, 0.0, v)

        @pl.loop(0, 4)
        def _(k):
            pair = pair_of(p, lax.rem(3 + 3 * k + 2 * (my_lev // 4) + my_row // 8, 4))
            at = pl.multiple_of(pair * 8, 8)
            groups = []
            for group in range(4):
                v = [work[pl.ds(pl.multiple_of((group * 4 + g) * 128 + at, 8), 8), :] for g in range(4)]
                groups.append(swap4(v, 32))
            for half in range(2):
                for q in range(4):
                    a, b = groups[half * 2][q], groups[half * 2 + 1][q]
                    send_a[at + q, half * 8:half * 8 + 8] = jnp.where(low, a, pltpu.roll(b, 4, 0))
                    send_a[at + 4 + q, half * 8:half * 8 + 8] = jnp.where(low, pltpu.roll(a, 4, 0), b)

            @pl.loop(0, 8)
            def _(e):
                other = at + lax.rem(6 + 7 * e + me, 8)

                @pl.when(other != me)
                def _():
                    pltpu.make_async_remote_copy(
                        send_a.at[other], recv_a.at[here], as_sem, ar_sem, device_id=place(other), device_id_type=MESH
                    ).start()

                @pl.when(other == me)
                def _():
                    pltpu.make_async_copy(send_a.at[me], recv_a.at[here], own_sem).start()

    def all_of(send, recv, ss, rs):
        return pltpu.make_async_remote_copy(
            send.at[pl.ds(0, N - 1)], recv.at[pl.ds(0, N - 1)], ss, rs,
            device_id=(my_lev, up_row), device_id_type=MESH,
        )

    for c in loads[5:]:
        c.wait()

    @pl.loop(0, 32, unroll=4)
    def _(y):
        mat_back[y] = jnp.concatenate(halves(mat[y]), axis=1)
        mat_fwd[y] = jnp.concatenate(halves(mat[y].T), axis=1)

    @pl.loop(0, 16, unroll=2)
    def _(u):
        at = pl.ds(pl.multiple_of(u * 128, 128), 128)
        t[at] = jnp.where(as_column(rcell[pl.ds(u, 1), :] & 127) == tile_lane, 1.0, 0.0)
        rows = as_column(rcell[pl.ds(u, 1), :] >> 7)
        for k in range(16):
            hot[at, k * 128:k * 128 + 128] = one_hot(rows == tile_lane + k * 128)

    @pl.loop(0, 16, unroll=2)
    def _(u):
        at = pl.ds(pl.multiple_of(u * 128, 128), 128)
        rows = tile_row + u * 128
        for k in range(16):
            hot_turned[at, k * 128:k * 128 + 128] = one_hot((rcell[k:k + 1, :] >> 7) == rows)

    pltpu.make_async_copy(send_a.at[me], recv_a.at[here], own_sem).wait()
    flow = all_of(send_a, recv_a, as_sem, ar_sem)
    flow.wait_recv()

    @pl.loop(0, 16, unroll=2)
    def _(j):
        v = recv_a[pl.ds(j * 8, 8)].reshape(128, 128).T
        for r, u in enumerate(swap4([v[g * 32:g * 32 + 32] for g in range(4)], 1)):
            cols[pl.ds(pl.multiple_of((j * 4 + r) * PITCH, 8), 32), :] = u

    @pl.loop(0, 32, unroll=4)
    def _(y):
        v = dot_split(cols[pl.ds(y, 64, stride=PITCH), :], mat_fwd[y])
        at = pl.ds(pl.multiple_of(y * 64, 64), 64)
        field[at] = v
        h, l = halves(v)
        parts[at, 0:128] = h
        parts[at, 128:256] = l

    final_copy = pltpu.make_async_copy(field, final_out, out_sem.at[0])
    final_copy.start()

    def product(a, b):
        g = jnp.zeros((a.shape[0], 256), F32)
        for k in range(8):
            g = g + dot(a[:, k * 256:k * 256 + 256], b[k * 256:k * 256 + 256], ((1,), (0,)))
        return g[:, :128] + g[:, 128:]

    def place_in_rows(g, mask, base, out):
        g = jnp.sum(jnp.where(mask, g, 0.0), axis=1, keepdims=True)
        for s in range(g.shape[0] // 128):
            out[pl.ds(base + s, 1), :] = as_row(g[s * 128:s * 128 + 128])

    @pl.loop(0, 2)
    def _(u):
        at = pl.ds(pl.multiple_of(u * TILE, TILE), TILE)
        place_in_rows(product(hot.at[at], parts), t[at] != 0.0, u * 8, picked)

    crossing = jax.nn.sigmoid(2.0 * (picked[...] - rlim[...]))
    cross[...] = crossing
    cross_copy = pltpu.make_async_copy(cross, cross_out, out_sem.at[2])
    cross_copy.start()
    picked[...] = 2.0 * crossing * (1.0 - crossing)

    @pl.loop(0, 16, unroll=2)
    def _(u):
        at = pl.ds(pl.multiple_of(u * 128, 128), 128)
        h, l = halves(t[at] * as_column(picked[pl.ds(u, 1), :]))
        values[at, 0:128] = h
        values[at, 128:256] = l

    @pl.loop(0, 2)
    def _(u):
        at = pl.ds(pl.multiple_of(u * TILE, TILE), TILE)
        work[at] = product(hot_turned.at[at], values)

    @pl.loop(0, 32, unroll=4)
    def _(y):
        at = pl.ds(pl.multiple_of(y * 64, 64), 64)
        cols[pl.ds(y, 64, stride=PITCH), :] = dot_split(work[at], mat_back[y])

    flow.wait_send()

    def far_strip(k):
        return 4 * lax.rem(my_row // 4 + 2 + 3 * (k // 4), 4) + lax.rem(my_row + 2 + 3 * k, 4)

    def send_back(w, j, n):
        i = piece(w) + 4 * lax.rem(my_lev // 4 + 1 + n, 2)
        block = j * N_LEV + i
        at_home = (i == my_lev) & (j == my_row)

        @pl.when(jnp.logical_not(at_home))
        def _():
            pltpu.make_async_remote_copy(
                send_a.at[block], recv_b.at[me], bs_sem.at[w], br_sem.at[w], device_id=(i, j), device_id_type=MESH
            ).start()

        @pl.when(at_home)
        def _():
            pltpu.make_async_copy(send_a.at[here], recv_b.at[me], own_sem).start()

    @pl.loop(0, 16)
    def _(k):
        j = far_strip(k)
        v = [cols[pl.ds(pl.multiple_of((j * 4 + r) * PITCH, 8), 32), :] for r in range(4)]
        v = jnp.concatenate(swap4(v, 1), axis=0).T
        send_a[pl.ds(j * 8, 8)] = v.reshape(8, 16, 128)

        for n in range(2):
            send_back(0, j, n)

    @pl.loop(1, 4)
    def _(w):
        @pl.loop(0, 16)
        def _(k):
            for n in range(2):
                send_back(w, far_strip(k), n)

    for s in range(4):
        c = scell[s:s + 1, :]
        at = pl.ds(s * 128, 128)
        cols[at] = jnp.where(as_column(c & 127) == tile_lane, 1.0, 0.0)
        rows = as_column((c >> 14) * 128 + ((c >> 7) & 31) * 4 + ((c >> 12) & 3))
        for k in range(16):
            hot[at, k * 128:k * 128 + 128] = one_hot(rows == tile_lane + k * 128)

    def wave(w, n):
        return pltpu.make_async_remote_copy(
            send_a.at[pl.ds(0, n)], recv_b.at[pl.ds(0, n)], bs_sem.at[w], br_sem.at[w],
            device_id=(my_lev, up_row), device_id_type=MESH,
        )

    pltpu.make_async_copy(send_a.at[here], recv_b.at[me], own_sem).wait()
    for w in range(4):
        wave(w, 31 if w == 0 else 32).wait_recv()
        p = piece(w)

        @pl.loop(0, 4)
        def _(k):
            at = pl.multiple_of(pair_of(p, k) * 8, 8)
            for half in range(2):
                va, vb = [], []
                for q in range(4):
                    u = recv_b[at + q, half * 8:half * 8 + 8]
                    s = recv_b[at + 4 + q, half * 8:half * 8 + 8]
                    va.append(jnp.where(low, u, pltpu.roll(s, 4, 0)))
                    vb.append(jnp.where(low, pltpu.roll(u, 4, 0), s))
                for group, v in ((half * 2, va), (half * 2 + 1, vb)):
                    for g, u in enumerate(swap4(v, 32)):
                        t[pl.ds(pl.multiple_of((group * 4 + g) * 128 + at, 8), 8), :] = u

        for lev in range(16):
            for half in range(2):
                e, at = edge_rows(lev, half, p, 3)
                hback_send[0, p, at] = jnp.where(sx[e, :] != 0, 0.0, cx[e, :] * t[e, :])
                e, at = edge_rows(lev, half, p, 0)
                hback_send[1, p, at] = jnp.where(sx[e, :] != 0, cx[e, :] * t[e, :], 0.0)
        for slot in range(2):
            exchange(hback_send, hback_recv, 2, slot, p).start()

    @pl.loop(0, 16)
    def _(lev):
        at = pl.ds(pl.multiple_of(lev * 128, 128), 128)
        v, a, b = t[at], cx[at], cy[at]
        flux_x, flux_y = a * v, b * v
        lower_x, lower_y = sx[at] != 0, sy[at] != 0
        work[at] = (
            (1.0 - a - b) * v
            + from_after(jnp.where(lower_x, flux_x, 0.0))
            + from_before(jnp.where(lower_x, 0.0, flux_x))
            + from_right(jnp.where(lower_y, flux_y, 0.0))
            + from_left(jnp.where(lower_y, 0.0, flux_y))
        )

    for p in range(4):
        for slot in range(2):
            exchange(hback_send, hback_recv, 2, slot, p).wait()

    def edge_of(slot):
        v = exchange_halves(hback_recv[slot, 0], hback_recv[slot, 1])
        u = exchange_halves(hback_recv[slot, 2], hback_recv[slot, 3])
        v = (v[0], u[0], v[1], u[1])
        return jnp.concatenate([x[lev * 8:lev * 8 + 8] for lev in range(16) for x in v], axis=0)

    first = pl.ds(0, 512, stride=4)
    final = pl.ds(3, 512, stride=4)
    work[first, :] = work[first, :] + has_down * edge_of(0)
    work[final, :] = work[final, :] + has_up * edge_of(1)
    adj_copy = pltpu.make_async_copy(work, adj_out, out_sem.at[1])
    adj_copy.start()

    @pl.loop(0, 16)
    def _(lev):
        at = pl.ds(pl.multiple_of(lev * 128, 128), 128)
        h, l = halves(work[at])
        parts[at, 0:128] = h
        parts[at, 128:256] = l

    place_in_rows(product(hot.at[pl.ds(0, 512)], parts), cols[0:512] != 0.0, 0, picked)
    stack_values = picked[0:4, :] * swt[...]
    partial = jnp.zeros((128, 256), F32)
    wide = iota((128, 256), 1)
    for s in range(4):
        owner = one_hot(sdest[s:s + 1, :] == tile_row)
        slot = as_column(sslot[s:s + 1, :])
        amount = as_column(stack_values[s:s + 1, :])
        slot = jnp.concatenate([slot, slot], axis=1)
        amount = jnp.concatenate([amount, amount], axis=1)
        h, l = halves(jnp.where(slot == wide, amount, 0.0))
        partial = partial + (dot(owner, h, ((1,), (0,))) + dot(owner, l, ((1,), (0,))))
    core = lax.rem(my_lev, 2)
    core_send[...] = partial.reshape(4, 2, N_ROW, 256)
    other_core = (2 * my_y + 1 - core, my_row)
    swap = pltpu.make_async_remote_copy(
        core_send.at[:, 1 - core], core_recv, ps_sem, pr_sem, device_id=other_core, device_id_type=MESH
    )
    swap.start()
    swap.wait_recv()
    total = (core_send[:, core] + core_recv[...]).reshape(64, 256)
    owner_send[:, 0, :] = total[:, :128]
    owner_send[:, 1, :] = total[:, 128:]
    here = my_y * N_ROW + my_row
    owner_recv[here] = owner_send[here]

    for dy in (2, 1, 3, 0):
        y = lax.rem(my_y + dy, 4)

        @pl.loop(0, 16)
        def _(k):
            row = far_strip(k)

            @pl.when(y * N_ROW + row != here)
            def _():
                pltpu.make_async_remote_copy(
                    owner_send.at[y * N_ROW + row], owner_recv.at[here], cs_sem, cr_sem,
                    device_id=(2 * y + core, row), device_id_type=MESH,
                ).start()

    last = pltpu.make_async_remote_copy(
        owner_send.at[pl.ds(0, 63)], owner_recv.at[pl.ds(0, 63)], cs_sem, cr_sem,
        device_id=other_core, device_id_type=MESH,
    )
    last.wait_recv()
    inv[...] = jnp.sum(owner_recv[...], axis=0)
    inv_copy = pltpu.make_async_copy(inv, inv_out, out_sem.at[3])
    inv_copy.start()
    swap.wait_send()
    last.wait_send()
    for w in range(4):
        wave(w, 31 if w == 0 else 32).wait_send()
    final_copy.wait()
    adj_copy.wait()
    cross_copy.wait()
    inv_copy.wait()


def write_out(*refs):
    stages = [], []
    for a, b, held in zip(refs[:4], refs[4:8], refs[8:12]):
        rows = a.shape[0]
        step = min(rows, 512)
        for at in range(0, rows, step):
            for n, (src, dst) in enumerate(((a, held), (held, b))):
                here = pl.ds(at, step)
                stages[n].append(pltpu.make_async_copy(src.at[here], dst.at[here], refs[12].at[n, len(stages[n])]))
    for c in stages[0]:
        c.start()
    for c, d in zip(*stages):
        c.wait()
        d.start()
    for d in stages[1]:
        d.wait()


def rows_of(slab):
    return slab.reshape(16, 4, 32, 128).transpose(0, 2, 1, 3).reshape(ROWS, 128)


def local(
    tracer, courant_x, courant_y, wind_x, wind_y, inverse_diffusion,
    receptor_cell, receptor_limit, stack_cell, stack_dest, stack_slot, stack_weight,
):
    hbm = pl.BlockSpec(memory_space=pl.ANY)
    slab = pltpu.VMEM((ROWS, 128), F32)
    dma = pltpu.SemaphoreType.DMA
    blocks = pltpu.VMEM((N, 16, 128), F32)
    edge = pltpu.VMEM((2, 4, 128, 128), F32)
    results = pl.pallas_call(
        kernel,
        out_shape=(
            jax.ShapeDtypeStruct((ROWS, 128), F32),
            jax.ShapeDtypeStruct((16, 128), F32),
            jax.ShapeDtypeStruct((ROWS, 128), F32),
            jax.ShapeDtypeStruct((2, 128), F32),
        ),
        in_specs=[hbm] * 12,
        out_specs=(hbm,) * 4,
        scratch_shapes=[
            slab, slab, slab, pltpu.VMEM((ROWS, 128), I32), pltpu.VMEM((ROWS, 128), I32), pltpu.VMEM((32, 128, 128), F32),
            pltpu.VMEM((16, 128), I32), pltpu.VMEM((16, 128), F32), pltpu.VMEM((4, 128), I32), pltpu.VMEM((4, 128), I32),
            pltpu.VMEM((4, 128), I32), pltpu.VMEM((4, 128), F32), pltpu.VMEM((16, 128), F32), pltpu.VMEM((2, 128), F32),
            pltpu.VMEM((32, 128, 256), BF16), pltpu.VMEM((32, 128, 256), BF16),
            pltpu.VMEM((ROWS, ROWS), BF16), pltpu.VMEM((ROWS, ROWS), BF16),
            slab, pltpu.VMEM((64 * PITCH, 128), F32), slab, pltpu.VMEM((ROWS, 256), BF16),
            pltpu.VMEM((ROWS, 256), BF16), blocks, blocks, blocks,
            pltpu.VMEM((64, 2, 128), F32), pltpu.VMEM((64, 2, 128), F32),
            pltpu.VMEM((4, 2, N_ROW, 256), F32), pltpu.VMEM((4, N_ROW, 256), F32),
            edge, edge, edge, edge, pltpu.VMEM((16, 128), F32),
            dma((12,)), dma, dma((4,)), dma((4, 4)), dma((4, 4)), dma, dma, dma((4,)), dma((4,)), dma, dma, dma, dma, pltpu.SemaphoreType.REGULAR,
        ],
        compiler_params=pltpu.CompilerParams(
            collective_id=0, has_side_effects=True, vmem_limit_bytes=56 * 1024 * 1024
        ),
        name="transport",
    )(
        rows_of(tracer), rows_of(courant_x), rows_of(courant_y), rows_of(wind_x), rows_of(wind_y), inverse_diffusion,
        receptor_cell.reshape(16, 128), receptor_limit.reshape(16, 128), stack_cell.reshape(4, 128),
        stack_dest.reshape(4, 128), stack_slot.reshape(4, 128), stack_weight.reshape(4, 128),
    )
    final_field, crossing, adjoint, inventory = pl.pallas_call(
        write_out,
        out_shape=tuple(jax.ShapeDtypeStruct(r.shape, r.dtype) for r in results),
        in_specs=[hbm] * 4,
        out_specs=(hbm,) * 4,
        scratch_shapes=[pltpu.VMEM(r.shape, r.dtype) for r in results] + [dma((2, 10))],
        name="write_out",
    )(*results)
    adjoint = adjoint.reshape(16, 32, 4, 128).transpose(0, 2, 1, 3).reshape(16, 4, 4096)
    return final_field.reshape(32, 64, 128), crossing.reshape(-1), adjoint, inventory.reshape(-1)


def solution(mesh):
    slab = P("lev", "row", None)
    flat = P(("lev", "row"))
    return jax.shard_map(
        local,
        mesh=mesh,
        in_specs=(slab,) * 5 + (P(("lev", "row"), None, None), flat, flat, flat, P(("lev", "row"), None), flat, flat),
        out_specs=(P(("lev", "row"), None, None), flat, slab, flat),
        check_vma=False,
    )
```

```python
import functools

import jax
import jax.numpy as jnp
from jax import lax
from jax.experimental import pallas as pl
from jax.experimental.pallas import tpu as pltpu
from jax.sharding import PartitionSpec as P

F32 = jnp.float32
BF16 = jnp.bfloat16
I32 = jnp.int32
MESH = pl.DeviceIdType.MESH
N_LEV = 8
N_ROW = 16
N = N_LEV * N_ROW
ROWS = 2048
PITCH = 40
TILE = 1024


def place(d):
    return (d // N_ROW, lax.rem(d, N_ROW))


def iota(shape, dim):
    return lax.broadcasted_iota(I32, shape, dim)


def swap4(v, unit):
    lane = iota(v[0].shape, 1)
    for bit in (1, 2):
        step = unit * bit
        high = (lane & step) != 0
        out = list(v)
        for a in range(4):
            if a & bit:
                continue
            b = a | bit
            out[a] = jnp.where(high, pltpu.roll(v[b], step, 1), v[a])
            out[b] = jnp.where(high, v[b], pltpu.roll(v[a], 128 - step, 1))
        v = out
    return v


def as_column(row):
    return jnp.broadcast_to(row, (128, 128)).T


def as_row(column):
    eye = iota((128, 128), 0) == iota((128, 128), 1)
    return jnp.sum(jnp.where(eye, jnp.broadcast_to(column, (128, 128)), 0.0), axis=0, keepdims=True)


def halves(v):
    high = v.astype(BF16)
    return high, (v - high.astype(F32)).astype(BF16)


def dot(a, b, dims):
    return lax.dot_general(a, b, (dims, ((), ())), preferred_element_type=F32)


def dot_split(a, b):
    n = a.shape[0]
    g = dot(jnp.concatenate(halves(a), axis=0), b, ((1,), (0,)))
    return (g[:n, :128] + g[n:, :128]) + (g[:n, 128:] + g[n:, 128:])


def one_hot(mask):
    return jnp.where(mask, 1.0, 0.0).astype(BF16)


def kernel(
    t_in, cx_in, cy_in, sx_in, sy_in, mat_in, rcell_in, rlim_in, scell_in, sdest_in, sslot_in, swt_in,
    final_out, cross_out, adj_out, inv_out,
    t, cx, cy, sx, sy, mat, rcell, rlim, scell, sdest, sslot, swt, cross, inv,
    mat_fwd, mat_back, hot, hot_turned, work, cols, field, parts, values, send_a, recv_a, recv_b, owner_send, owner_recv, core_send, core_recv,
    halo_send, halo_recv, hback_send, hback_recv, picked,
    load_sem, own_sem, out_sem, hs_sem, hr_sem, as_sem, ar_sem, bs_sem, br_sem, cs_sem, cr_sem, ps_sem, pr_sem, ready,
):
    my_lev = lax.axis_index("lev")
    my_row = lax.axis_index("row")
    my_y = my_lev // 2
    me = my_lev * N_ROW + my_row
    up_row = lax.rem(my_row + 1, N_ROW)
    down_row = lax.rem(my_row + N_ROW - 1, N_ROW)

    loads = []
    inputs = (
        (t_in, t), (cx_in, cx), (cy_in, cy), (sx_in, sx), (sy_in, sy), (mat_in, mat), (rcell_in, rcell),
        (rlim_in, rlim), (scell_in, scell), (sdest_in, sdest), (sslot_in, sslot), (swt_in, swt),
    )
    for n, (src, dst) in enumerate(inputs):
        c = pltpu.make_async_copy(src, dst, load_sem.at[n])
        c.start()
        loads.append(c)

    barrier = pltpu.get_barrier_semaphore()

    @pl.loop(1, N_ROW)
    def _(k):
        other = (my_lev, lax.rem(my_row + k, N_ROW))
        pl.semaphore_signal(barrier, inc=1, device_id=other, device_id_type=MESH)

    @pl.loop(1, N_LEV)
    def _(k):
        other = (lax.rem(my_lev + k, N_LEV), my_row)
        pl.semaphore_signal(barrier, inc=1, device_id=other, device_id_type=MESH)

    loads[0].wait()
    tile_row = iota((128, 128), 0)
    tile_lane = iota((128, 128), 1)
    tile_low = (tile_row & 4) == 0

    def exchange_halves(a, b):
        return jnp.where(tile_low, a, pltpu.roll(b, 4, 0)), jnp.where(tile_low, pltpu.roll(a, 124, 0), b)

    for slot, start in ((0, 3), (1, 0)):
        edge = t[pl.ds(start, 512, stride=4), :].reshape(16, 4, 8, 128)
        for n in range(2):
            a, b = exchange_halves(edge[:, n].reshape(128, 128), edge[:, n + 2].reshape(128, 128))
            halo_send[slot, 2 * n] = a
            halo_send[slot, 2 * n + 1] = b

    def piece(w):
        return 2 * lax.rem(my_lev // 2 + w // 2, 2) + lax.rem(my_lev + w, 2)

    def pair_of(p, n):
        return 2 * p + lax.rem(n, 2) + 8 * (n // 2)

    pl.semaphore_wait(barrier, N_ROW + N_LEV - 2)

    @pl.loop(1, N_ROW)
    def _(k):
        other = (my_lev, lax.rem(my_row + k, N_ROW))
        pl.semaphore_signal(ready, inc=1, device_id=other, device_id_type=MESH)


    def exchange(send, recv, base, slot, p):
        return pltpu.make_async_remote_copy(
            send.at[slot, p], recv.at[slot, p], hs_sem.at[base + slot, p], hr_sem.at[base + slot, p],
            device_id=(my_lev, (up_row, down_row)[slot]), device_id_type=MESH,
        )

    @pl.loop(0, 4)
    def _(w):
        for slot in range(2):
            exchange(halo_send, halo_recv, 0, slot, piece(w)).start()

    for c in loads[1:5]:
        c.wait()

    strip_row = tile_row & 3

    def from_left(v):
        rolled = pltpu.roll(v, 1, 1)
        carried = jnp.where(tile_row < 4, 0.0, pltpu.roll(rolled, 4, 0))
        return jnp.where(tile_lane == 0, carried, rolled)

    def from_right(v):
        rolled = pltpu.roll(v, 127, 1)
        carried = jnp.where(tile_row >= 124, 0.0, pltpu.roll(rolled, 124, 0))
        return jnp.where(tile_lane == 127, carried, rolled)

    def from_before(v):
        return jnp.where(strip_row == 0, 0.0, pltpu.roll(v, 1, 0))

    def from_after(v):
        return jnp.where(strip_row == 3, 0.0, pltpu.roll(v, 127, 0))

    @pl.loop(0, 16)
    def _(lev):
        at = pl.ds(pl.multiple_of(lev * 128, 128), 128)
        v, a, b = t[at], cx[at], cy[at]
        work[at] = (
            (1.0 - a - b) * v
            + a * jnp.where(sx[at] != 0, from_before(v), from_after(v))
            + b * jnp.where(sy[at] != 0, from_left(v), from_right(v))
        )

    has_down = jnp.where(my_row > 0, 1.0, 0.0)
    has_up = jnp.where(my_row < N_ROW - 1, 1.0, 0.0)

    def edge_rows(lev, half, p, r):
        return pl.ds(lev * 128 + half * 64 + p * 16 + r, 4, stride=4), pl.ds(lev * 8 + half * 4, 4)

    pl.semaphore_wait(ready, N_ROW - 1)

    low = iota((8, 128), 0) < 4
    here = my_row * N_LEV + my_lev

    @pl.loop(0, 4)
    def _(w):
        p = piece(w)
        for slot in range(2):
            exchange(halo_send, halo_recv, 0, slot, p).wait()
        for lev in range(16):
            for half in range(2):
                e, at = edge_rows(lev, half, p, 0)
                v = cx[e, :] * halo_recv[0, p, at]
                work[e, :] = work[e, :] + has_down * jnp.where(sx[e, :] != 0, v, 0.0)
                e, at = edge_rows(lev, half, p, 3)
                v = cx[e, :] * halo_recv[1, p, at]
                work[e, :] = work[e, :] + has_up * jnp.where(sx[e, :] != 0, 0.0, v)

        @pl.loop(0, 4)
        def _(k):
            pair = pair_of(p, lax.rem(3 + 3 * k + 2 * (my_lev // 4) + my_row // 8, 4))
            at = pl.multiple_of(pair * 8, 8)
            groups = []
            for group in range(4):
                v = [work[pl.ds(pl.multiple_of((group * 4 + g) * 128 + at, 8), 8), :] for g in range(4)]
                groups.append(swap4(v, 32))
            for half in range(2):
                for q in range(4):
                    a, b = groups[half * 2][q], groups[half * 2 + 1][q]
                    send_a[at + q, half * 8:half * 8 + 8] = jnp.where(low, a, pltpu.roll(b, 4, 0))
                    send_a[at + 4 + q, half * 8:half * 8 + 8] = jnp.where(low, pltpu.roll(a, 4, 0), b)

            @pl.loop(0, 8)
            def _(e):
                other = at + lax.rem(6 + 7 * e + me, 8)

                @pl.when(other != me)
                def _():
                    pltpu.make_async_remote_copy(
                        send_a.at[other], recv_a.at[here], as_sem, ar_sem, device_id=place(other), device_id_type=MESH
                    ).start()

                @pl.when(other == me)
                def _():
                    pltpu.make_async_copy(send_a.at[me], recv_a.at[here], own_sem).start()

    def all_of(send, recv, ss, rs):
        return pltpu.make_async_remote_copy(
            send.at[pl.ds(0, N - 1)], recv.at[pl.ds(0, N - 1)], ss, rs,
            device_id=(my_lev, up_row), device_id_type=MESH,
        )

    for c in loads[5:]:
        c.wait()

    @pl.loop(0, 32, unroll=4)
    def _(y):
        mat_back[y] = jnp.concatenate(halves(mat[y]), axis=1)
        mat_fwd[y] = jnp.concatenate(halves(mat[y].T), axis=1)

    @pl.loop(0, 16, unroll=2)
    def _(u):
        at = pl.ds(pl.multiple_of(u * 128, 128), 128)
        t[at] = jnp.where(as_column(rcell[pl.ds(u, 1), :] & 127) == tile_lane, 1.0, 0.0)
        rows = as_column(rcell[pl.ds(u, 1), :] >> 7)
        for k in range(16):
            hot[at, k * 128:k * 128 + 128] = one_hot(rows == tile_lane + k * 128)

    @pl.loop(0, 16, unroll=2)
    def _(u):
        at = pl.ds(pl.multiple_of(u * 128, 128), 128)
        rows = tile_row + u * 128
        for k in range(16):
            hot_turned[at, k * 128:k * 128 + 128] = one_hot((rcell[k:k + 1, :] >> 7) == rows)

    pltpu.make_async_copy(send_a.at[me], recv_a.at[here], own_sem).wait()
    flow = all_of(send_a, recv_a, as_sem, ar_sem)
    flow.wait_recv()

    @pl.loop(0, 16, unroll=4)
    def _(j):
        v = recv_a[pl.ds(j * 8, 8)].reshape(128, 128).T
        for r, u in enumerate(swap4([v[g * 32:g * 32 + 32] for g in range(4)], 1)):
            cols[pl.ds(pl.multiple_of((j * 4 + r) * PITCH, 8), 32), :] = u

    @pl.loop(0, 32, unroll=8)
    def _(y):
        v = dot_split(cols[pl.ds(y, 64, stride=PITCH), :], mat_fwd[y])
        at = pl.ds(pl.multiple_of(y * 64, 64), 64)
        field[at] = v
        h, l = halves(v)
        parts[at, 0:128] = h
        parts[at, 128:256] = l

    final_copy = pltpu.make_async_copy(field, final_out, out_sem.at[0])
    final_copy.start()

    def product(a, b):
        g = jnp.zeros((a.shape[0], 256), F32)
        for k in range(8):
            g = g + dot(a[:, k * 256:k * 256 + 256], b[k * 256:k * 256 + 256], ((1,), (0,)))
        return g[:, :128] + g[:, 128:]

    def place_in_rows(g, mask, base, out):
        g = jnp.sum(jnp.where(mask, g, 0.0), axis=1, keepdims=True)
        for s in range(g.shape[0] // 128):
            out[pl.ds(base + s, 1), :] = as_row(g[s * 128:s * 128 + 128])

    @pl.loop(0, 2)
    def _(u):
        at = pl.ds(pl.multiple_of(u * TILE, TILE), TILE)
        place_in_rows(product(hot.at[at], parts), t[at] != 0.0, u * 8, picked)

    crossing = jax.nn.sigmoid(2.0 * (picked[...] - rlim[...]))
    cross[...] = crossing
    cross_copy = pltpu.make_async_copy(cross, cross_out, out_sem.at[2])
    cross_copy.start()
    picked[...] = 2.0 * crossing * (1.0 - crossing)

    @pl.loop(0, 16, unroll=2)
    def _(u):
        at = pl.ds(pl.multiple_of(u * 128, 128), 128)
        h, l = halves(t[at] * as_column(picked[pl.ds(u, 1), :]))
        values[at, 0:128] = h
        values[at, 128:256] = l

    @pl.loop(0, 2)
    def _(u):
        at = pl.ds(pl.multiple_of(u * TILE, TILE), TILE)
        work[at] = product(hot_turned.at[at], values)

    @pl.loop(0, 32, unroll=8)
    def _(y):
        at = pl.ds(pl.multiple_of(y * 64, 64), 64)
        cols[pl.ds(y, 64, stride=PITCH), :] = dot_split(work[at], mat_back[y])

    flow.wait_send()

    def far_strip(k):
        return 4 * lax.rem(my_row // 4 + 2 + 3 * (k // 4), 4) + lax.rem(my_row + 2 + 3 * k, 4)

    def send_back(w, j, n):
        i = piece(w) + 4 * lax.rem(my_lev // 4 + 1 + n, 2)
        block = j * N_LEV + i
        at_home = (i == my_lev) & (j == my_row)

        @pl.when(jnp.logical_not(at_home))
        def _():
            pltpu.make_async_remote_copy(
                send_a.at[block], recv_b.at[me], bs_sem.at[w], br_sem.at[w], device_id=(i, j), device_id_type=MESH
            ).start()

        @pl.when(at_home)
        def _():
            pltpu.make_async_copy(send_a.at[here], recv_b.at[me], own_sem).start()

    @pl.loop(0, 16)
    def _(k):
        j = far_strip(k)
        v = [cols[pl.ds(pl.multiple_of((j * 4 + r) * PITCH, 8), 32), :] for r in range(4)]
        v = jnp.concatenate(swap4(v, 1), axis=0).T
        send_a[pl.ds(j * 8, 8)] = v.reshape(8, 16, 128)

        for n in range(2):
            send_back(0, j, n)

    @pl.loop(1, 4)
    def _(w):
        @pl.loop(0, 16)
        def _(k):
            for n in range(2):
                send_back(w, far_strip(k), n)

    for s in range(4):
        c = scell[s:s + 1, :]
        at = pl.ds(s * 128, 128)
        cols[at] = jnp.where(as_column(c & 127) == tile_lane, 1.0, 0.0)
        rows = as_column((c >> 14) * 128 + ((c >> 7) & 31) * 4 + ((c >> 12) & 3))
        for k in range(16):
            hot[at, k * 128:k * 128 + 128] = one_hot(rows == tile_lane + k * 128)

    def wave(w, n):
        return pltpu.make_async_remote_copy(
            send_a.at[pl.ds(0, n)], recv_b.at[pl.ds(0, n)], bs_sem.at[w], br_sem.at[w],
            device_id=(my_lev, up_row), device_id_type=MESH,
        )

    pltpu.make_async_copy(send_a.at[here], recv_b.at[me], own_sem).wait()
    for w in range(4):
        wave(w, 31 if w == 0 else 32).wait_recv()
        p = piece(w)

        @pl.loop(0, 4, unroll=2)
        def _(k):
            at = pl.multiple_of(pair_of(p, k) * 8, 8)
            for half in range(2):
                va, vb = [], []
                for q in range(4):
                    u = recv_b[at + q, half * 8:half * 8 + 8]
                    s = recv_b[at + 4 + q, half * 8:half * 8 + 8]
                    va.append(jnp.where(low, u, pltpu.roll(s, 4, 0)))
                    vb.append(jnp.where(low, pltpu.roll(u, 4, 0), s))
                for group, v in ((half * 2, va), (half * 2 + 1, vb)):
                    for g, u in enumerate(swap4(v, 32)):
                        t[pl.ds(pl.multiple_of((group * 4 + g) * 128 + at, 8), 8), :] = u

        for lev in range(16):
            for half in range(2):
                e, at = edge_rows(lev, half, p, 3)
                hback_send[0, p, at] = jnp.where(sx[e, :] != 0, 0.0, cx[e, :] * t[e, :])
                e, at = edge_rows(lev, half, p, 0)
                hback_send[1, p, at] = jnp.where(sx[e, :] != 0, cx[e, :] * t[e, :], 0.0)
        for slot in range(2):
            exchange(hback_send, hback_recv, 2, slot, p).start()

    @pl.loop(0, 16)
    def _(lev):
        at = pl.ds(pl.multiple_of(lev * 128, 128), 128)
        v, a, b = t[at], cx[at], cy[at]
        flux_x, flux_y = a * v, b * v
        lower_x, lower_y = sx[at] != 0, sy[at] != 0
        work[at] = (
            (1.0 - a - b) * v
            + from_after(jnp.where(lower_x, flux_x, 0.0))
            + from_before(jnp.where(lower_x, 0.0, flux_x))
            + from_right(jnp.where(lower_y, flux_y, 0.0))
            + from_left(jnp.where(lower_y, 0.0, flux_y))
        )

    for p in range(4):
        for slot in range(2):
            exchange(hback_send, hback_recv, 2, slot, p).wait()

    def edge_of(slot):
        v = exchange_halves(hback_recv[slot, 0], hback_recv[slot, 1])
        u = exchange_halves(hback_recv[slot, 2], hback_recv[slot, 3])
        v = (v[0], u[0], v[1], u[1])
        return jnp.concatenate([x[lev * 8:lev * 8 + 8] for lev in range(16) for x in v], axis=0)

    first = pl.ds(0, 512, stride=4)
    final = pl.ds(3, 512, stride=4)
    work[first, :] = work[first, :] + has_down * edge_of(0)
    work[final, :] = work[final, :] + has_up * edge_of(1)
    adj_copy = pltpu.make_async_copy(work, adj_out, out_sem.at[1])
    adj_copy.start()

    @pl.loop(0, 16)
    def _(lev):
        at = pl.ds(pl.multiple_of(lev * 128, 128), 128)
        h, l = halves(work[at])
        parts[at, 0:128] = h
        parts[at, 128:256] = l

    place_in_rows(product(hot.at[pl.ds(0, 512)], parts), cols[0:512] != 0.0, 0, picked)
    stack_values = picked[0:4, :] * swt[...]
    partial = jnp.zeros((128, 256), F32)
    wide = iota((128, 256), 1)
    for s in range(4):
        owner = one_hot(sdest[s:s + 1, :] == tile_row)
        slot = as_column(sslot[s:s + 1, :])
        amount = as_column(stack_values[s:s + 1, :])
        slot = jnp.concatenate([slot, slot], axis=1)
        amount = jnp.concatenate([amount, amount], axis=1)
        h, l = halves(jnp.where(slot == wide, amount, 0.0))
        partial = partial + (dot(owner, h, ((1,), (0,))) + dot(owner, l, ((1,), (0,))))
    core = lax.rem(my_lev, 2)
    core_send[...] = partial.reshape(4, 2, N_ROW, 256)
    other_core = (2 * my_y + 1 - core, my_row)
    swap = pltpu.make_async_remote_copy(
        core_send.at[:, 1 - core], core_recv, ps_sem, pr_sem, device_id=other_core, device_id_type=MESH
    )
    swap.start()
    swap.wait_recv()
    total = (core_send[:, core] + core_recv[...]).reshape(64, 256)
    owner_send[:, 0, :] = total[:, :128]
    owner_send[:, 1, :] = total[:, 128:]
    here = my_y * N_ROW + my_row
    owner_recv[here] = owner_send[here]

    for dy in (2, 1, 3, 0):
        y = lax.rem(my_y + dy, 4)

        @pl.loop(0, 16)
        def _(k):
            row = far_strip(k)

            @pl.when(y * N_ROW + row != here)
            def _():
                pltpu.make_async_remote_copy(
                    owner_send.at[y * N_ROW + row], owner_recv.at[here], cs_sem, cr_sem,
                    device_id=(2 * y + core, row), device_id_type=MESH,
                ).start()

    last = pltpu.make_async_remote_copy(
        owner_send.at[pl.ds(0, 63)], owner_recv.at[pl.ds(0, 63)], cs_sem, cr_sem,
        device_id=other_core, device_id_type=MESH,
    )
    last.wait_recv()
    inv[...] = jnp.sum(owner_recv[...], axis=0)
    inv_copy = pltpu.make_async_copy(inv, inv_out, out_sem.at[3])
    inv_copy.start()
    swap.wait_send()
    last.wait_send()
    for w in range(4):
        wave(w, 31 if w == 0 else 32).wait_send()
    final_copy.wait()
    adj_copy.wait()
    cross_copy.wait()
    inv_copy.wait()


def write_out(*refs):
    stages = [], []
    for a, b, held in zip(refs[:4], refs[4:8], refs[8:12]):
        rows = a.shape[0]
        step = min(rows, 512)
        for at in range(0, rows, step):
            for n, (src, dst) in enumerate(((a, held), (held, b))):
                here = pl.ds(at, step)
                stages[n].append(pltpu.make_async_copy(src.at[here], dst.at[here], refs[12].at[n, len(stages[n])]))
    for c in stages[0]:
        c.start()
    for c, d in zip(*stages):
        c.wait()
        d.start()
    for d in stages[1]:
        d.wait()


def rows_of(slab):
    return slab.reshape(16, 4, 32, 128).transpose(0, 2, 1, 3).reshape(ROWS, 128)


def local(
    tracer, courant_x, courant_y, wind_x, wind_y, inverse_diffusion,
    receptor_cell, receptor_limit, stack_cell, stack_dest, stack_slot, stack_weight,
):
    hbm = pl.BlockSpec(memory_space=pl.ANY)
    slab = pltpu.VMEM((ROWS, 128), F32)
    dma = pltpu.SemaphoreType.DMA
    blocks = pltpu.VMEM((N, 16, 128), F32)
    edge = pltpu.VMEM((2, 4, 128, 128), F32)
    results = pl.pallas_call(
        kernel,
        out_shape=(
            jax.ShapeDtypeStruct((ROWS, 128), F32),
            jax.ShapeDtypeStruct((16, 128), F32),
            jax.ShapeDtypeStruct((ROWS, 128), F32),
            jax.ShapeDtypeStruct((2, 128), F32),
        ),
        in_specs=[hbm] * 12,
        out_specs=(hbm,) * 4,
        scratch_shapes=[
            slab, slab, slab, pltpu.VMEM((ROWS, 128), I32), pltpu.VMEM((ROWS, 128), I32), pltpu.VMEM((32, 128, 128), F32),
            pltpu.VMEM((16, 128), I32), pltpu.VMEM((16, 128), F32), pltpu.VMEM((4, 128), I32), pltpu.VMEM((4, 128), I32),
            pltpu.VMEM((4, 128), I32), pltpu.VMEM((4, 128), F32), pltpu.VMEM((16, 128), F32), pltpu.VMEM((2, 128), F32),
            pltpu.VMEM((32, 128, 256), BF16), pltpu.VMEM((32, 128, 256), BF16),
            pltpu.VMEM((ROWS, ROWS), BF16), pltpu.VMEM((ROWS, ROWS), BF16),
            slab, pltpu.VMEM((64 * PITCH, 128), F32), slab, pltpu.VMEM((ROWS, 256), BF16),
            pltpu.VMEM((ROWS, 256), BF16), blocks, blocks, blocks,
            pltpu.VMEM((64, 2, 128), F32), pltpu.VMEM((64, 2, 128), F32),
            pltpu.VMEM((4, 2, N_ROW, 256), F32), pltpu.VMEM((4, N_ROW, 256), F32),
            edge, edge, edge, edge, pltpu.VMEM((16, 128), F32),
            dma((12,)), dma, dma((4,)), dma((4, 4)), dma((4, 4)), dma, dma, dma((4,)), dma((4,)), dma, dma, dma, dma, pltpu.SemaphoreType.REGULAR,
        ],
        compiler_params=pltpu.CompilerParams(
            collective_id=0, has_side_effects=True, vmem_limit_bytes=56 * 1024 * 1024
        ),
        name="transport",
    )(
        rows_of(tracer), rows_of(courant_x), rows_of(courant_y), rows_of(wind_x), rows_of(wind_y), inverse_diffusion,
        receptor_cell.reshape(16, 128), receptor_limit.reshape(16, 128), stack_cell.reshape(4, 128),
        stack_dest.reshape(4, 128), stack_slot.reshape(4, 128), stack_weight.reshape(4, 128),
    )
    final_field, crossing, adjoint, inventory = pl.pallas_call(
        write_out,
        out_shape=tuple(jax.ShapeDtypeStruct(r.shape, r.dtype) for r in results),
        in_specs=[hbm] * 4,
        out_specs=(hbm,) * 4,
        scratch_shapes=[pltpu.VMEM(r.shape, r.dtype) for r in results] + [dma((2, 10))],
        name="write_out",
    )(*results)
    adjoint = adjoint.reshape(16, 32, 4, 128).transpose(0, 2, 1, 3).reshape(16, 4, 4096)
    return final_field.reshape(32, 64, 128), crossing.reshape(-1), adjoint, inventory.reshape(-1)


def solution(mesh):
    slab = P("lev", "row", None)
    flat = P(("lev", "row"))
    return jax.shard_map(
        local,
        mesh=mesh,
        in_specs=(slab,) * 5 + (P(("lev", "row"), None, None), flat, flat, flat, P(("lev", "row"), None), flat, flat),
        out_specs=(P(("lev", "row"), None, None), flat, slab, flat),
        check_vma=False,
    )
```
